32 devices in a mesh: outer: 8 (over z, y), inner: 4 (over x, core).
Axes of the slice: x: 2, y: 2, z: 4, core: 2. Of those that a mesh axis runs over, the one named last changes fastest.
Arguments:
- query_states: bfloat16 [4096, 4096], P(('outer', 'inner')), may hold values from -6 to 6
- key_states: bfloat16 [4096, 4096], P(('outer', 'inner')), may hold values from -6 to 6
- value_states: bfloat16 [4096, 4096], P(('outer', 'inner')), may hold values from -6 to 6
- doc_lengths: int32 [8], replicated, may hold values from 1 to 1024, 4096 in all
- slopes: float32 [32], replicated, may hold values from 0.00024414062 to 0.0625
Outputs:
- attended: bfloat16 [4096, 4096], P(('outer', 'inner'))
The draws below stay inside these ranges and needn't reach their ends.
Inputs may be any that keep to these rules, and one draw needn't show every extreme that they name: `doc_lengths`: the lengths add up to 4096; the longest is exactly 1024.
All inputs are finite; a program needn't handle non-finite values.
Results may differ from the reference program's by a relative error of at most 0.0045.
Values may be sent and summed in bfloat16 or wider, within the bound.
A program may use at most 64 MiB of HBM per device.

```python
import math
import jax
import jax.numpy as jnp
import numpy as np
from jax import lax

H = 32
HD = 128
TOK_DEV = 128
TOKENS = 4096
DOC_MAX = 1024
DOCS = 8


def paired_draw(key):
    shape = (TOKENS, H * HD)
    query_key = jax.random.fold_in(key, 7001)
    second_key = jax.random.fold_in(key, 7002)
    row_ids = jnp.arange(TOKENS)[:, None]
    query_part = jnp.clip(jax.random.normal(query_key, shape, jnp.float32), -5.5, 5.5)
    key_part = jnp.clip(jax.random.normal(second_key, shape, jnp.float32), -5.5, 5.5)
    reach = DOC_MAX // 2
    far_signs = jax.random.rademacher(jax.random.fold_in(key, 7005), shape).astype(jnp.float32)
    far_vector = 5.5 * far_signs
    far_query = row_ids % 61 == 20
    query_part = jnp.where(far_query, far_vector, query_part)
    partner_row = row_ids + reach
    far_key = (partner_row % 61 == 20) & (partner_row < TOKENS)
    key_part = jnp.where(far_key, jnp.roll(far_vector, -reach, axis=0), key_part)
    return (query_part, key_part)


def draw_query_states(key, part):
    return paired_draw(key)[0].astype(jnp.bfloat16)


def draw_key_states(key, part):
    return paired_draw(key)[1].astype(jnp.bfloat16)


def draw_slopes(key, part):
    lowest = jnp.float32(0.25 / DOC_MAX)
    highest = jnp.float32(0.0625)
    fraction = jax.random.uniform(jax.random.fold_in(key, 7010), (H,), jnp.float32)
    return jnp.exp(jnp.log(lowest) + fraction * (jnp.log(highest) - jnp.log(lowest)))


def steps_of(key, shape, cuts, low, high):
    gain = 1.0
    for position, shards_of in cuts:
        steps = jax.random.uniform(jax.random.fold_in(jax.random.fold_in(key, 6), position), (shards_of,), jnp.float32, low / len(cuts), high / len(cuts))
        gain = gain * jnp.repeat(jnp.exp(steps), shape[position] // shards_of).reshape((-1,) + (1,) * (len(shape) - 1 - position))
    return gain


def length_profile(amount, total, most, lean):
    loads = [(1 << 20) // math.isqrt(grade ** lean) + 1 for grade in range(2, amount + 1)]
    rest, counts = total - most - (amount - 1), [1] * (amount - 1)
    while rest > 0:
        free = [i for i in range(amount - 1) if counts[i] < most]
        whole, left = sum([loads[i] for i in free]), rest
        for i in free:
            extra = min(most - counts[i], max(1, left * loads[i] // whole), rest)
            counts[i] = counts[i] + extra
            rest = rest - extra
    return np.array([most] + counts)


def ragged_sizes(stream_key, number_of, total, limit, slope):
    if number_of == 2:
        one = jax.random.randint(stream_key, (), max(1, total - limit), min(limit, total - 1) + 1)
        return jnp.stack([one, total - one])
    lengths = jnp.asarray(length_profile(number_of, total, limit, slope), jnp.int32)
    couples = (number_of - 1) // 2
    donor, taker = lengths[1:1 + 2 * couples:2], lengths[2:2 + 2 * couples:2]
    room = jnp.minimum(donor - 1, limit - taker)
    passed = jax.random.randint(jax.random.fold_in(stream_key, 1), (couples,), 0, 1 << 20) % (room + 1)
    lengths = lengths.at[1:1 + 2 * couples:2].set(donor - passed).at[2:2 + 2 * couples:2].set(taker + passed)
    return lengths[jax.random.permutation(jax.random.fold_in(stream_key, 2), number_of)]


def scatter_about(key, shape, spread, most, cuts=(), kind=jnp.bfloat16):
    result = spread * jax.random.normal(key, shape, jnp.float32)
    if cuts:
        result = result * steps_of(key, shape, cuts, -0.22, 0.18)
    return jnp.clip(result, -most, most).astype(kind)


def setup_inputs(seed: int = 0) -> dict:
    key_list = jax.random.split(jax.random.key(seed), 6)
    return {
        "query_states": draw_query_states(jax.random.fold_in(key_list[5], 71), 0),
        "key_states": draw_key_states(jax.random.fold_in(key_list[5], 71), 0),
        "value_states": scatter_about(key_list[2], (TOKENS, H * HD), 1.0, 6.0, ((0, 32),)),
        "doc_lengths": ragged_sizes(key_list[3], DOCS, TOKENS, DOC_MAX, 2).astype(jnp.int32),
        "slopes": draw_slopes(jax.random.fold_in(key_list[5], 71), 0),
    }


NEG_FILL = -1e+30

def reference(query_states, key_states, value_states, doc_lengths, slopes):
    boundary = jnp.cumsum(doc_lengths).astype(jnp.int32)
    positions = jnp.arange(TOKENS, dtype=jnp.int32)
    doc_index = lax.optimization_barrier(jnp.sum((boundary[None, :] <= positions[:, None]).astype(jnp.int32), axis=1))
    queries_all = query_states.reshape(TOKENS, H, HD)
    padded_keys = jnp.concatenate([jnp.zeros((DOC_MAX, H, HD), key_states.dtype), key_states.reshape(TOKENS, H, HD)], axis=0)
    padded_values = jnp.concatenate([jnp.zeros((DOC_MAX, H, HD), value_states.dtype), value_states.reshape(TOKENS, H, HD)], axis=0)
    padded_pos = jnp.arange(TOKENS + DOC_MAX, dtype=jnp.int32) - DOC_MAX
    padded_doc = jnp.concatenate([jnp.full((DOC_MAX,), -1, jnp.int32), doc_index])
    block_rows = 256 if TOKENS % 256 == 0 else TOK_DEV
    window = DOC_MAX + block_rows
    inv_root = 1.0 / math.sqrt(HD)

    def one_block(block_id):
        row_start = (block_id * block_rows).astype(jnp.int32)
        query_block = lax.dynamic_slice_in_dim(queries_all, row_start, block_rows, 0).astype(jnp.float32)
        query_pos = lax.dynamic_slice_in_dim(positions, row_start, block_rows, 0)
        query_doc = lax.dynamic_slice_in_dim(doc_index, row_start, block_rows, 0)
        key_block = lax.dynamic_slice_in_dim(padded_keys, row_start, window, 0).astype(jnp.float32)
        value_block = lax.dynamic_slice_in_dim(padded_values, row_start, window, 0).astype(jnp.float32)
        key_pos = lax.dynamic_slice_in_dim(padded_pos, row_start, window, 0)
        key_doc = lax.dynamic_slice_in_dim(padded_doc, row_start, window, 0)
        scores = jnp.einsum('qhd,khd->qhk', query_block, key_block, precision=lax.Precision.HIGHEST) * inv_root
        distance = (query_pos[:, None] - key_pos[None, :]).astype(jnp.float32)
        scores = scores - slopes[None, :, None] * distance[:, None, :]
        allowed = (query_doc[:, None] == key_doc[None, :]) & (key_pos[None, :] <= query_pos[:, None])
        scores = jnp.where(allowed[:, None, :], scores, NEG_FILL)
        row_max = lax.optimization_barrier(jnp.max(scores, axis=-1))
        weights = jnp.where(allowed[:, None, :], jnp.exp(scores - row_max[:, :, None]), 0.0)
        row_total = lax.optimization_barrier(jnp.sum(weights, axis=-1))
        rounded = lax.optimization_barrier(weights.astype(jnp.bfloat16)).astype(jnp.float32)
        numerator = jnp.einsum('qhk,khd->qhd', rounded, value_block, precision=lax.Precision.HIGHEST)
        return (numerator / row_total[:, :, None]).astype(jnp.bfloat16).reshape(block_rows, H * HD)
    blocks = lax.map(one_block, jnp.arange(TOKENS // block_rows, dtype=jnp.int32))
    return blocks.reshape(TOKENS, H * HD)
```

```python
import functools
import math

import jax
import jax.numpy as jnp
from jax import lax
from jax.experimental import pallas as pl
from jax.experimental.pallas import tpu as pltpu
from jax.sharding import PartitionSpec as P

DOC_MAX = 1024
BLOCK = 256
NEG_FILL = -1e30
LOG2E = math.log2(math.e)
MESH = pl.DeviceIdType.MESH


def kernel(
    plane_groups, inner_count, planes, heads, width,
    doc_ref, slope_ref, q_ref, k_ref, v_ref, out_ref,
    q_buf, k_buf, v_buf, o_buf, start_buf,
    in_send, in_recv, z_send, z_recv, out_send, out_recv,
):
    rows = q_ref.shape[0]
    slots = plane_groups * inner_count
    outer = lax.axis_index("outer")
    inner = lax.axis_index("inner")
    plane = outer // plane_groups
    slot = (outer % plane_groups) * inner_count + inner
    has_prev = plane > 0
    has_next = plane < planes - 1
    prev_id = {"outer": outer - plane_groups, "inner": inner}
    next_id = {"outer": outer + plane_groups, "inner": inner}

    def peer_of(step):
        peer = (slot + step) % slots
        return peer, {"outer": plane * plane_groups + peer // inner_count, "inner": peer % inner_count}

    def columns(owner, head):
        return pl.ds(pl.multiple_of((owner * heads + head) * width, width), width)

    own_rows = pl.ds(pl.multiple_of(slot * rows, rows), rows)
    home_rows = pl.ds(pl.multiple_of(DOC_MAX + slot * rows, rows), rows)

    barrier = pltpu.get_barrier_semaphore()
    for step in range(1, slots):
        pl.semaphore_signal(barrier, inc=1, device_id=peer_of(step)[1], device_id_type=MESH)

    @pl.when(has_prev)
    def _():
        pl.semaphore_signal(barrier, inc=1, device_id=prev_id, device_id_type=MESH)

    @pl.when(has_next)
    def _():
        pl.semaphore_signal(barrier, inc=1, device_id=next_id, device_id_type=MESH)

    pl.semaphore_wait(barrier, slots - 1 + has_prev.astype(jnp.int32) + has_next.astype(jnp.int32))

    tensors = ((k_ref, k_buf, home_rows), (v_ref, v_buf, home_rows), (q_ref, q_buf, own_rows))
    for head in range(heads):
        for kind, (source, target, place) in enumerate(tensors):
            for step in range(1, slots):
                peer, peer_id = peer_of(step)
                pltpu.make_async_remote_copy(
                    src_ref=source.at[:, columns(peer, head)],
                    dst_ref=target.at[head, place, :],
                    send_sem=in_send.at[kind],
                    recv_sem=in_recv.at[kind, head],
                    device_id=peer_id,
                    device_id_type=MESH,
                ).start()
            pltpu.make_async_copy(
                source.at[:, columns(slot, head)], target.at[head, place, :], in_recv.at[kind, head]
            ).start()

    @pl.when(jnp.logical_not(has_prev))
    def _():
        k_buf[:, :DOC_MAX, :] = jnp.zeros((heads, DOC_MAX, width), k_buf.dtype)
        v_buf[:, :DOC_MAX, :] = jnp.zeros((heads, DOC_MAX, width), v_buf.dtype)

    position = plane * DOC_MAX + lax.broadcasted_iota(jnp.int32, (DOC_MAX, 1), 0)

    def next_document(index, carry):
        end, start = carry
        end = end + doc_ref[index]
        return end, jnp.where(position >= end, end, start)

    start = lax.fori_loop(
        0, doc_ref.shape[0], next_document, (jnp.int32(0), jnp.zeros((DOC_MAX, 1), jnp.int32))
    )[1]
    start_buf[...] = (start - (plane - 1) * DOC_MAX).astype(jnp.float32)

    def whole(ref, sem):
        return pltpu.make_async_copy(ref, ref, sem)

    def forward(head):
        for kind, buf in enumerate((k_buf, v_buf)):
            whole(buf.at[head, pl.ds(DOC_MAX, DOC_MAX), :], in_recv.at[kind, head]).wait()

            @pl.when(has_next)
            def _():
                pltpu.make_async_remote_copy(
                    src_ref=buf.at[head, pl.ds(DOC_MAX, DOC_MAX), :],
                    dst_ref=buf.at[head, pl.ds(0, DOC_MAX), :],
                    send_sem=z_send.at[kind, head],
                    recv_sem=z_recv.at[kind, head],
                    device_id=next_id,
                    device_id_type=MESH,
                ).start()

    window = DOC_MAX + BLOCK

    def attend(head):
        whole(q_buf.at[head], in_recv.at[2, head]).wait()

        @pl.when(has_prev)
        def _():
            for kind, buf in enumerate((k_buf, v_buf)):
                whole(buf.at[head, pl.ds(0, DOC_MAX), :], z_recv.at[kind, head]).wait()

        slope = slope_ref[slot * heads + head] * LOG2E
        scale = LOG2E / math.sqrt(width)

        def one_block(index, unused):
            first = pl.multiple_of(index * BLOCK, BLOCK)
            query = q_buf[head, pl.ds(first, BLOCK), :]
            keys = k_buf[head, pl.ds(first, window), :]
            values = v_buf[head, pl.ds(first, window), :]
            scores = lax.dot_general(
                query, keys, (((1,), (1,)), ((), ())), preferred_element_type=jnp.float32
            )
            key_pos = lax.broadcasted_iota(jnp.int32, (1, window), 1).astype(jnp.float32)
            query_pos = (lax.broadcasted_iota(jnp.int32, (BLOCK, 1), 0) + DOC_MAX).astype(jnp.float32)
            earliest = start_buf[pl.ds(first, BLOCK), :] - first.astype(jnp.float32)
            allowed = (key_pos >= earliest) & (key_pos <= query_pos)
            scores = jnp.where(allowed, scores * scale + slope * key_pos, NEG_FILL)
            row_max = jnp.max(scores, axis=1, keepdims=True)
            weights = jnp.exp2(scores - row_max)
            row_total = jnp.sum(weights, axis=1, keepdims=True)
            numerator = jnp.dot(
                weights.astype(jnp.bfloat16), values, preferred_element_type=jnp.float32
            )
            o_buf[head, pl.ds(first, BLOCK), :] = (numerator / row_total).astype(o_buf.dtype)
            return unused

        lax.fori_loop(0, DOC_MAX // BLOCK, one_block, 0)
        for step in range(1, slots):
            peer, peer_id = peer_of(step)
            pltpu.make_async_remote_copy(
                src_ref=o_buf.at[head, pl.ds(pl.multiple_of(peer * rows, rows), rows), :],
                dst_ref=out_ref.at[:, columns(slot, head)],
                send_sem=out_send,
                recv_sem=out_recv,
                device_id=peer_id,
                device_id_type=MESH,
            ).start()
        pltpu.make_async_copy(
            o_buf.at[head, own_rows, :], out_ref.at[:, columns(slot, head)], out_recv
        ).start()

    forward(0)
    for head in range(1, heads):
        forward(head)
        attend(head - 1)
    attend(heads - 1)

    sent = pl.ds(0, (slots - 1) * heads * width)
    for kind, (source, unused, place) in enumerate(tensors):
        whole(source.at[:, sent], in_send.at[kind]).wait()
    whole(out_ref.at[:, sent], out_send).wait()

    @pl.when(has_next)
    def _():
        for head in range(heads):
            for kind, buf in enumerate((k_buf, v_buf)):
                whole(buf.at[head, pl.ds(DOC_MAX, DOC_MAX), :], z_send.at[kind, head]).wait()

    whole(out_ref, out_recv).wait()


def per_device(query_states, key_states, value_states, doc_lengths, slopes):
    rows, all_columns = query_states.shape
    width = all_columns // slopes.shape[0]
    inner_count = lax.axis_size("inner")
    plane_groups = DOC_MAX // (rows * inner_count)
    slots = plane_groups * inner_count
    planes = lax.axis_size("outer") // plane_groups
    heads = slopes.shape[0] // slots
    dtype = query_states.dtype
    return pl.pallas_call(
        functools.partial(kernel, plane_groups, inner_count, planes, heads, width),
        out_shape=jax.ShapeDtypeStruct((rows, all_columns), dtype),
        in_specs=[pl.BlockSpec(memory_space=pltpu.SMEM)] * 2 + [pl.BlockSpec(memory_space=pl.ANY)] * 3,
        out_specs=pl.BlockSpec(memory_space=pl.ANY),
        scratch_shapes=[
            pltpu.VMEM((heads, DOC_MAX, width), dtype),
            pltpu.VMEM((heads, 2 * DOC_MAX, width), dtype),
            pltpu.VMEM((heads, 2 * DOC_MAX, width), dtype),
            pltpu.VMEM((heads, DOC_MAX, width), dtype),
            pltpu.VMEM((DOC_MAX, 1), jnp.float32),
            pltpu.SemaphoreType.DMA((3,)),
            pltpu.SemaphoreType.DMA((3, heads)),
            pltpu.SemaphoreType.DMA((2, heads)),
            pltpu.SemaphoreType.DMA((2, heads)),
            pltpu.SemaphoreType.DMA,
            pltpu.SemaphoreType.DMA,
        ],
        compiler_params=pltpu.CompilerParams(
            collective_id=0, has_side_effects=True, vmem_limit_bytes=48 * 1024 * 1024
        ),
        cost_estimate=pl.CostEstimate(
            flops=4 * heads * DOC_MAX * (DOC_MAX + BLOCK) * width,
            bytes_accessed=8 * rows * all_columns,
            transcendentals=heads * DOC_MAX * (DOC_MAX + BLOCK),
        ),
    )(doc_lengths, slopes, query_states, key_states, value_states)


def solution(mesh):
    placed = P(("outer", "inner"), None)
    return jax.shard_map(
        per_device,
        mesh=mesh,
        in_specs=(placed, placed, placed, P(), P()),
        out_specs=placed,
        check_vma=False,
    )
```

```python
import functools
import math

import jax
import jax.numpy as jnp
from jax import lax
from jax.experimental import pallas as pl
from jax.experimental.pallas import tpu as pltpu
from jax.sharding import PartitionSpec as P

DOC_MAX = 1024
BLOCK = 256
NEG_FILL = -1e30
LOG2E = math.log2(math.e)
MESH = pl.DeviceIdType.MESH


def kernel(
    plane_groups, inner_count, planes, heads, width,
    doc_hbm, slope_hbm, q_ref, k_ref, v_ref, out_ref,
    doc_ref, slope_ref, q_buf, k_buf, v_buf, o_buf, start_buf,
    small_sem, in_send, in_recv, z_send, z_recv, out_send, out_recv,
):
    rows = q_ref.shape[0]
    slots = plane_groups * inner_count
    outer = lax.axis_index("outer")
    inner = lax.axis_index("inner")
    plane = outer // plane_groups
    slot = (outer % plane_groups) * inner_count + inner
    has_prev = plane > 0
    has_next = plane < planes - 1
    prev_id = {"outer": outer - plane_groups, "inner": inner}
    next_id = {"outer": outer + plane_groups, "inner": inner}

    def peer_of(step):
        peer = (slot + step) % slots
        return peer, {"outer": plane * plane_groups + peer // inner_count, "inner": peer % inner_count}

    def columns(owner, head):
        return pl.ds(pl.multiple_of((owner * heads + head) * width, width), width)

    own_rows = pl.ds(pl.multiple_of(slot * rows, rows), rows)
    home_rows = pl.ds(pl.multiple_of(DOC_MAX + slot * rows, rows), rows)

    small = [
        pltpu.make_async_copy(doc_hbm, doc_ref, small_sem.at[0]),
        pltpu.make_async_copy(slope_hbm, slope_ref, small_sem.at[1]),
    ]
    for copy in small:
        copy.start()

    barrier = pltpu.get_barrier_semaphore()
    for step in range(1, slots):
        pl.semaphore_signal(barrier, inc=1, device_id=peer_of(step)[1], device_id_type=MESH)

    @pl.when(has_prev)
    def _():
        pl.semaphore_signal(barrier, inc=1, device_id=prev_id, device_id_type=MESH)

    @pl.when(has_next)
    def _():
        pl.semaphore_signal(barrier, inc=1, device_id=next_id, device_id_type=MESH)

    pl.semaphore_wait(barrier, slots - 1 + has_prev.astype(jnp.int32) + has_next.astype(jnp.int32))

    tensors = ((k_ref, k_buf, home_rows), (v_ref, v_buf, home_rows), (q_ref, q_buf, own_rows))
    for head in range(heads):
        for kind, (source, target, place) in enumerate(tensors):
            for step in range(1, slots):
                peer, peer_id = peer_of(step)
                pltpu.make_async_remote_copy(
                    src_ref=source.at[:, columns(peer, head)],
                    dst_ref=target.at[head, place, :],
                    send_sem=in_send.at[kind],
                    recv_sem=in_recv.at[kind, head],
                    device_id=peer_id,
                    device_id_type=MESH,
                ).start()
            pltpu.make_async_copy(
                source.at[:, columns(slot, head)], target.at[head, place, :], in_recv.at[kind, head]
            ).start()

    @pl.when(jnp.logical_not(has_prev))
    def _():
        k_buf[:, :DOC_MAX, :] = jnp.zeros((heads, DOC_MAX, width), k_buf.dtype)
        v_buf[:, :DOC_MAX, :] = jnp.zeros((heads, DOC_MAX, width), v_buf.dtype)

    for copy in small:
        copy.wait()

    position = plane * DOC_MAX + lax.broadcasted_iota(jnp.int32, (DOC_MAX, 1), 0)

    def next_document(index, carry):
        end, start = carry
        end = end + doc_ref[index]
        return end, jnp.where(position >= end, end, start)

    start = lax.fori_loop(
        0, doc_ref.shape[0], next_document, (jnp.int32(0), jnp.zeros((DOC_MAX, 1), jnp.int32))
    )[1]
    start_buf[...] = (start - (plane - 1) * DOC_MAX).astype(jnp.float32)

    def whole(ref, sem):
        return pltpu.make_async_copy(ref, ref, sem)

    def forward(head):
        for kind, buf in enumerate((k_buf, v_buf)):
            whole(buf.at[head, pl.ds(DOC_MAX, DOC_MAX), :], in_recv.at[kind, head]).wait()

            @pl.when(has_next)
            def _():
                pltpu.make_async_remote_copy(
                    src_ref=buf.at[head, pl.ds(DOC_MAX, DOC_MAX), :],
                    dst_ref=buf.at[head, pl.ds(0, DOC_MAX), :],
                    send_sem=z_send.at[kind, head],
                    recv_sem=z_recv.at[kind, head],
                    device_id=next_id,
                    device_id_type=MESH,
                ).start()

    window = DOC_MAX + BLOCK

    def attend(head):
        whole(q_buf.at[head], in_recv.at[2, head]).wait()

        @pl.when(has_prev)
        def _():
            for kind, buf in enumerate((k_buf, v_buf)):
                whole(buf.at[head, pl.ds(0, DOC_MAX), :], z_recv.at[kind, head]).wait()

        slope = slope_ref[slot * heads + head] * LOG2E
        scale = LOG2E / math.sqrt(width)

        def one_block(index, unused):
            first = pl.multiple_of(index * BLOCK, BLOCK)
            query = q_buf[head, pl.ds(first, BLOCK), :]
            keys = k_buf[head, pl.ds(first, window), :]
            values = v_buf[head, pl.ds(first, window), :]
            scores = lax.dot_general(
                query, keys, (((1,), (1,)), ((), ())), preferred_element_type=jnp.float32
            )
            key_pos = lax.broadcasted_iota(jnp.int32, (1, window), 1).astype(jnp.float32)
            query_pos = (lax.broadcasted_iota(jnp.int32, (BLOCK, 1), 0) + DOC_MAX).astype(jnp.float32)
            earliest = start_buf[pl.ds(first, BLOCK), :] - first.astype(jnp.float32)
            allowed = (key_pos >= earliest) & (key_pos <= query_pos)
            scores = jnp.where(allowed, scores * scale + slope * key_pos, NEG_FILL)
            row_max = jnp.max(scores, axis=1, keepdims=True)
            weights = jnp.exp2(scores - row_max)
            row_total = jnp.sum(weights, axis=1, keepdims=True)
            numerator = jnp.dot(
                weights.astype(jnp.bfloat16), values, preferred_element_type=jnp.float32
            )
            o_buf[head, pl.ds(first, BLOCK), :] = (numerator / row_total).astype(o_buf.dtype)

            for part in range(BLOCK // rows):
                peer = index * (BLOCK // rows) + part
                done_rows = o_buf.at[head, pl.ds(pl.multiple_of(peer * rows, rows), rows), :]

                @pl.when(peer != slot)
                def _():
                    pltpu.make_async_remote_copy(
                        src_ref=done_rows,
                        dst_ref=out_ref.at[:, columns(slot, head)],
                        send_sem=out_send,
                        recv_sem=out_recv,
                        device_id={
                            "outer": plane * plane_groups + peer // inner_count,
                            "inner": peer % inner_count,
                        },
                        device_id_type=MESH,
                    ).start()

                @pl.when(peer == slot)
                def _():
                    pltpu.make_async_copy(
                        done_rows, out_ref.at[:, columns(slot, head)], out_recv
                    ).start()

            return unused

        lax.fori_loop(0, DOC_MAX // BLOCK, one_block, 0)

    forward(0)
    for head in range(1, heads):
        forward(head)
        attend(head - 1)
    attend(heads - 1)

    sent = pl.ds(0, (slots - 1) * heads * width)
    for kind, (source, unused, place) in enumerate(tensors):
        whole(source.at[:, sent], in_send.at[kind]).wait()
    whole(out_ref.at[:, sent], out_send).wait()

    @pl.when(has_next)
    def _():
        for head in range(heads):
            for kind, buf in enumerate((k_buf, v_buf)):
                whole(buf.at[head, pl.ds(DOC_MAX, DOC_MAX), :], z_send.at[kind, head]).wait()

    whole(out_ref, out_recv).wait()


def per_device(query_states, key_states, value_states, doc_lengths, slopes):
    rows, all_columns = query_states.shape
    width = all_columns // slopes.shape[0]
    inner_count = lax.axis_size("inner")
    plane_groups = DOC_MAX // (rows * inner_count)
    slots = plane_groups * inner_count
    planes = lax.axis_size("outer") // plane_groups
    heads = slopes.shape[0] // slots
    dtype = query_states.dtype
    return pl.pallas_call(
        functools.partial(kernel, plane_groups, inner_count, planes, heads, width),
        out_shape=jax.ShapeDtypeStruct((rows, all_columns), dtype),
        in_specs=[pl.BlockSpec(memory_space=pltpu.HBM)] * 5,
        out_specs=pl.BlockSpec(memory_space=pltpu.HBM),
        scratch_shapes=[
            pltpu.SMEM(doc_lengths.shape, doc_lengths.dtype),
            pltpu.SMEM(slopes.shape, slopes.dtype),
            pltpu.VMEM((heads, DOC_MAX, width), dtype),
            pltpu.VMEM((heads, 2 * DOC_MAX, width), dtype),
            pltpu.VMEM((heads, 2 * DOC_MAX, width), dtype),
            pltpu.VMEM((heads, DOC_MAX, width), dtype),
            pltpu.VMEM((DOC_MAX, 1), jnp.float32),
            pltpu.SemaphoreType.DMA((2,)),
            pltpu.SemaphoreType.DMA((3,)),
            pltpu.SemaphoreType.DMA((3, heads)),
            pltpu.SemaphoreType.DMA((2, heads)),
            pltpu.SemaphoreType.DMA((2, heads)),
            pltpu.SemaphoreType.DMA,
            pltpu.SemaphoreType.DMA,
        ],
        compiler_params=pltpu.CompilerParams(
            collective_id=0, has_side_effects=True, vmem_limit_bytes=64 * 1024 * 1024
        ),
        cost_estimate=pl.CostEstimate(
            flops=4 * heads * DOC_MAX * (DOC_MAX + BLOCK) * width,
            bytes_accessed=8 * rows * all_columns,
            transcendentals=heads * DOC_MAX * (DOC_MAX + BLOCK),
        ),
    )(doc_lengths, slopes, query_states, key_states, value_states)


def solution(mesh):
    placed = P(("outer", "inner"), None)
    return jax.shard_map(
        per_device,
        mesh=mesh,
        in_specs=(placed, placed, placed, P(), P()),
        out_specs=placed,
        check_vma=False,
    )
```

```python
import functools
import math

import jax
import jax.numpy as jnp
from jax import lax
from jax.experimental import pallas as pl
from jax.experimental.pallas import tpu as pltpu
from jax.sharding import PartitionSpec as P

DOC_MAX = 1024
BLOCK = 256
NEG_FILL = -1e30
LOG2E = math.log2(math.e)
MESH = pl.DeviceIdType.MESH


def kernel(
    plane_groups, inner_count, planes, heads, width,
    doc_hbm, slope_hbm, q_ref, k_ref, v_ref, out_ref,
    doc_ref, slope_ref, q_buf, k_buf, v_buf, vt_buf, o_buf,
    far_out, far_in, lse_out, lse_in, near_sum, near_max, near_total, start_buf, pos_buf,
    small_sem, in_send, in_recv, z_send, z_recv, out_send, out_recv,
):
    rows = q_ref.shape[0]
    slots = plane_groups * inner_count
    outer = lax.axis_index("outer")
    inner = lax.axis_index("inner")
    plane = outer // plane_groups
    slot = (outer % plane_groups) * inner_count + inner
    has_prev = plane > 0
    has_next = plane < planes - 1
    prev_id = {"outer": outer - plane_groups, "inner": inner}
    next_id = {"outer": outer + plane_groups, "inner": inner}

    def device_of(peer):
        return {"outer": plane * plane_groups + peer // inner_count, "inner": peer % inner_count}

    def columns(owner, head):
        return pl.ds(pl.multiple_of((owner * heads + head) * width, width), width)

    own_rows = pl.ds(pl.multiple_of(slot * rows, rows), rows)

    small = [
        pltpu.make_async_copy(doc_hbm, doc_ref, small_sem.at[0]),
        pltpu.make_async_copy(slope_hbm, slope_ref, small_sem.at[1]),
    ]
    for copy in small:
        copy.start()

    barrier = pltpu.get_barrier_semaphore()
    for step in range(1, slots):
        pl.semaphore_signal(
            barrier, inc=1, device_id=device_of((slot + step) % slots), device_id_type=MESH
        )

    @pl.when(has_prev)
    def _():
        pl.semaphore_signal(barrier, inc=1, device_id=prev_id, device_id_type=MESH)

    @pl.when(has_next)
    def _():
        pl.semaphore_signal(barrier, inc=1, device_id=next_id, device_id_type=MESH)

    pl.semaphore_wait(barrier, slots - 1 + has_prev.astype(jnp.int32) + has_next.astype(jnp.int32))

    def exchange(kind, source, target, head):
        for step in range(1, slots):
            peer = (slot + step) % slots
            pltpu.make_async_remote_copy(
                src_ref=source.at[:, columns(peer, head)],
                dst_ref=target.at[head, own_rows, :],
                send_sem=in_send.at[kind],
                recv_sem=in_recv.at[kind, head],
                device_id=device_of(peer),
                device_id_type=MESH,
            ).start()
        pltpu.make_async_copy(
            source.at[:, columns(slot, head)], target.at[head, own_rows, :], in_recv.at[kind, head]
        ).start()

    for head in range(heads):
        exchange(0, q_ref, q_buf, head)
    for head in range(heads):
        exchange(1, k_ref, k_buf, head)
        exchange(2, v_ref, v_buf, head)

    for copy in small:
        copy.wait()

    position = plane * DOC_MAX + lax.broadcasted_iota(jnp.int32, (1, 2 * DOC_MAX), 1)

    def next_document(index, carry):
        end, start = carry
        end = end + doc_ref[index]
        return end, jnp.where(position >= end, end, start)

    start = lax.fori_loop(
        0, doc_ref.shape[0], next_document, (jnp.int32(0), jnp.zeros((1, 2 * DOC_MAX), jnp.int32))
    )[1]
    start_buf[...] = (start - plane * DOC_MAX).astype(jnp.float32)
    pos_buf[...] = lax.broadcasted_iota(jnp.int32, (DOC_MAX, BLOCK), 0).astype(jnp.float32)

    def whole(ref, sem):
        return pltpu.make_async_copy(ref, ref, sem)

    def z_copy(kind, head, source, target, device_id):
        return pltpu.make_async_remote_copy(
            src_ref=source,
            dst_ref=target,
            send_sem=z_send.at[kind, head],
            recv_sem=z_recv.at[kind, head],
            device_id=device_id,
            device_id_type=MESH,
        )

    scale = LOG2E / math.sqrt(width)
    blocks = DOC_MAX // BLOCK

    def score(head, query_first, key_first, key_count, slope, shift):
        keys = k_buf[head, pl.ds(key_first, key_count), :]
        query = q_buf[head, pl.ds(query_first, BLOCK), :]
        product = lax.dot_general(
            keys, query, (((1,), (1,)), ((), ())), preferred_element_type=jnp.float32
        )
        key_pos = pos_buf[pl.ds(key_first, key_count), :]
        allowed = key_pos >= start_buf[:, pl.ds(query_first, BLOCK)]
        return product * scale + (slope * key_pos + shift), allowed

    def weighted(key_first, key_count, weights):
        return jnp.dot(
            vt_buf[:, pl.ds(key_first, key_count)],
            weights.astype(jnp.bfloat16),
            preferred_element_type=jnp.float32,
        )

    def far(head, slope):
        for index in range(blocks):
            first, count = index * BLOCK, DOC_MAX - index * BLOCK
            scores, allowed = score(head, DOC_MAX + first, first, count, slope, -DOC_MAX * slope)
            scores = jnp.where(allowed, scores, NEG_FILL)
            row_max = jnp.max(scores, axis=0, keepdims=True)
            weights = jnp.exp2(scores - row_max)
            row_total = jnp.sum(weights, axis=0, keepdims=True)
            part = weighted(first, count, weights) / row_total
            far_out[head, :, pl.ds(first, BLOCK)] = part.astype(far_out.dtype)
            lse_out[head, :, pl.ds(first, BLOCK)] = row_max + jnp.log2(row_total)

    def near(head, slope):
        for index in range(blocks):
            first = index * BLOCK
            scores, allowed = score(head, first, first, BLOCK, slope, 0.0)
            causal = lax.broadcasted_iota(jnp.int32, (BLOCK, BLOCK), 0) <= (
                lax.broadcasted_iota(jnp.int32, (BLOCK, BLOCK), 1)
            )
            pieces = [(first, BLOCK, jnp.where(allowed & causal, scores, NEG_FILL))]
            if index:
                scores, allowed = score(head, first, 0, first, slope, 0.0)
                pieces.append((0, first, jnp.where(allowed, scores, NEG_FILL)))
            row_max = functools.reduce(
                jnp.maximum, [jnp.max(piece, axis=0, keepdims=True) for _, _, piece in pieces]
            )
            row_total, total = 0.0, 0.0
            for key_first, key_count, piece in pieces:
                weights = jnp.exp2(piece - row_max)
                row_total = row_total + jnp.sum(weights, axis=0, keepdims=True)
                total = total + weighted(key_first, key_count, weights)
            near_sum[:, pl.ds(first, BLOCK)] = total
            near_max[:, pl.ds(first, BLOCK)] = row_max
            near_total[:, pl.ds(first, BLOCK)] = row_total

    def send_home(head, index):
        for part in range(BLOCK // rows):
            peer = index * (BLOCK // rows) + part
            done_rows = o_buf.at[head, pl.ds(peer * rows, rows), :]

            @pl.when(peer != slot)
            def _():
                pltpu.make_async_remote_copy(
                    src_ref=done_rows,
                    dst_ref=out_ref.at[:, columns(slot, head)],
                    send_sem=out_send,
                    recv_sem=out_recv,
                    device_id=device_of(peer),
                    device_id_type=MESH,
                ).start()

            @pl.when(peer == slot)
            def _():
                pltpu.make_async_copy(
                    done_rows, out_ref.at[:, columns(slot, head)], out_recv
                ).start()

    def finish(head):
        @pl.when(has_prev)
        def _():
            whole(far_in.at[head], z_recv.at[1, head]).wait()
            whole(lse_in.at[head], z_recv.at[2, head]).wait()

        for index in range(blocks):
            part = pl.ds(index * BLOCK, BLOCK)

            @pl.when(has_prev)
            def _():
                far_lse = lse_in[head, :, part]
                top = jnp.maximum(near_max[:, part], far_lse)
                near_scale = jnp.exp2(near_max[:, part] - top)
                far_scale = jnp.exp2(far_lse - top)
                inverse = 1.0 / (near_total[:, part] * near_scale + far_scale)
                merged = near_sum[:, part] * (near_scale * inverse)
                merged = merged + far_in[head, :, part].astype(jnp.float32) * (far_scale * inverse)
                o_buf[head, part, :] = merged.T.astype(o_buf.dtype)

            @pl.when(jnp.logical_not(has_prev))
            def _():
                alone = near_sum[:, part] / near_total[:, part]
                o_buf[head, part, :] = alone.T.astype(o_buf.dtype)

            send_home(head, index)

    def queries_back(head, unused):
        whole(q_buf.at[head, pl.ds(0, DOC_MAX), :], in_recv.at[0, head]).wait()

        @pl.when(has_prev)
        def _():
            z_copy(
                0, head,
                q_buf.at[head, pl.ds(0, DOC_MAX), :],
                q_buf.at[head, pl.ds(DOC_MAX, DOC_MAX), :],
                prev_id,
            ).start()

        return unused

    lax.fori_loop(0, heads, queries_back, 0)

    def one_head(head, unused):
        slope = slope_ref[slot * heads + head] * LOG2E
        whole(k_buf.at[head], in_recv.at[1, head]).wait()
        whole(v_buf.at[head], in_recv.at[2, head]).wait()
        vt_buf[...] = v_buf[head].T

        @pl.when(has_next)
        def _():
            whole(q_buf.at[head, pl.ds(DOC_MAX, DOC_MAX), :], z_recv.at[0, head]).wait()
            far(head, slope)
            z_copy(1, head, far_out.at[head], far_in.at[head], next_id).start()
            z_copy(2, head, lse_out.at[head], lse_in.at[head], next_id).start()

        @pl.when(head > 0)
        def _():
            finish(head - 1)

        near(head, slope)
        return unused

    lax.fori_loop(0, heads, one_head, 0)
    finish(heads - 1)

    sent = pl.ds(0, (slots - 1) * heads * width)
    for kind, source in enumerate((q_ref, k_ref, v_ref)):
        whole(source.at[:, sent], in_send.at[kind]).wait()
    whole(out_ref.at[:, sent], out_send).wait()
    for head in range(heads):

        @pl.when(has_prev)
        def _():
            whole(q_buf.at[head, pl.ds(0, DOC_MAX), :], z_send.at[0, head]).wait()

        @pl.when(has_next)
        def _():
            whole(far_out.at[head], z_send.at[1, head]).wait()
            whole(lse_out.at[head], z_send.at[2, head]).wait()

    whole(out_ref, out_recv).wait()


def per_device(query_states, key_states, value_states, doc_lengths, slopes):
    rows, all_columns = query_states.shape
    width = all_columns // slopes.shape[0]
    inner_count = lax.axis_size("inner")
    plane_groups = DOC_MAX // (rows * inner_count)
    slots = plane_groups * inner_count
    planes = lax.axis_size("outer") // plane_groups
    heads = slopes.shape[0] // slots
    dtype = query_states.dtype
    return pl.pallas_call(
        functools.partial(kernel, plane_groups, inner_count, planes, heads, width),
        out_shape=jax.ShapeDtypeStruct((rows, all_columns), dtype),
        in_specs=[pl.BlockSpec(memory_space=pltpu.HBM)] * 5,
        out_specs=pl.BlockSpec(memory_space=pltpu.HBM),
        scratch_shapes=[
            pltpu.SMEM(doc_lengths.shape, doc_lengths.dtype),
            pltpu.SMEM(slopes.shape, slopes.dtype),
            pltpu.VMEM((heads, 2 * DOC_MAX, width), dtype),
            pltpu.VMEM((heads, DOC_MAX, width), dtype),
            pltpu.VMEM((heads, DOC_MAX, width), dtype),
            pltpu.VMEM((width, DOC_MAX), dtype),
            pltpu.VMEM((heads, DOC_MAX, width), dtype),
            pltpu.VMEM((heads, width, DOC_MAX), dtype),
            pltpu.VMEM((heads, width, DOC_MAX), dtype),
            pltpu.VMEM((heads, 1, DOC_MAX), jnp.float32),
            pltpu.VMEM((heads, 1, DOC_MAX), jnp.float32),
            pltpu.VMEM((width, DOC_MAX), jnp.float32),
            pltpu.VMEM((1, DOC_MAX), jnp.float32),
            pltpu.VMEM((1, DOC_MAX), jnp.float32),
            pltpu.VMEM((1, 2 * DOC_MAX), jnp.float32),
            pltpu.VMEM((DOC_MAX, BLOCK), jnp.float32),
            pltpu.SemaphoreType.DMA((2,)),
            pltpu.SemaphoreType.DMA((3,)),
            pltpu.SemaphoreType.DMA((3, heads)),
            pltpu.SemaphoreType.DMA((3, heads)),
            pltpu.SemaphoreType.DMA((3, heads)),
            pltpu.SemaphoreType.DMA,
            pltpu.SemaphoreType.DMA,
        ],
        compiler_params=pltpu.CompilerParams(
            collective_id=0, has_side_effects=True, vmem_limit_bytes=64 * 1024 * 1024
        ),
        cost_estimate=pl.CostEstimate(
            flops=4 * heads * DOC_MAX * (DOC_MAX + BLOCK) * width,
            bytes_accessed=8 * rows * all_columns,
            transcendentals=heads * DOC_MAX * (DOC_MAX + BLOCK),
        ),
    )(doc_lengths, slopes, query_states, key_states, value_states)


def solution(mesh):
    placed = P(("outer", "inner"), None)
    return jax.shard_map(
        per_device,
        mesh=mesh,
        in_specs=(placed, placed, placed, P(), P()),
        out_specs=placed,
        check_vma=False,
    )
```

```python
import functools
import math

import jax
import jax.numpy as jnp
from jax import lax
from jax.experimental import pallas as pl
from jax.experimental.pallas import tpu as pltpu
from jax.sharding import PartitionSpec as P

DOC_MAX = 1024
BLOCK = 256
NEG_FILL = -1e30
LOG2E = math.log2(math.e)
MESH = pl.DeviceIdType.MESH


def kernel(
    plane_groups, inner_count, planes, heads, width,
    doc_hbm, slope_hbm, q_ref, k_ref, v_ref, out_ref,
    doc_ref, slope_ref, q_buf, k_buf, v_buf, vt_buf, o_buf,
    far_out, far_in, lse_out, lse_in, near_sum, near_max, near_total, start_buf, pos_buf,
    small_sem, in_send, in_recv, z_send, z_recv, out_send, out_recv,
):
    rows = q_ref.shape[0]
    slots = plane_groups * inner_count
    outer = lax.axis_index("outer")
    inner = lax.axis_index("inner")
    plane = outer // plane_groups
    slot = (outer % plane_groups) * inner_count + inner
    has_prev = plane > 0
    has_next = plane < planes - 1
    prev_id = {"outer": outer - plane_groups, "inner": inner}
    next_id = {"outer": outer + plane_groups, "inner": inner}

    def device_of(peer):
        return {"outer": plane * plane_groups + peer // inner_count, "inner": peer % inner_count}

    def columns(owner, head):
        return pl.ds(pl.multiple_of((owner * heads + head) * width, width), width)

    own_rows = pl.ds(pl.multiple_of(slot * rows, rows), rows)

    small = [
        pltpu.make_async_copy(doc_hbm, doc_ref, small_sem.at[0]),
        pltpu.make_async_copy(slope_hbm, slope_ref, small_sem.at[1]),
    ]
    for copy in small:
        copy.start()

    barrier = pltpu.get_barrier_semaphore()
    for step in range(1, slots):
        pl.semaphore_signal(
            barrier, inc=1, device_id=device_of((slot + step) % slots), device_id_type=MESH
        )

    @pl.when(has_prev)
    def _():
        pl.semaphore_signal(barrier, inc=1, device_id=prev_id, device_id_type=MESH)

    @pl.when(has_next)
    def _():
        pl.semaphore_signal(barrier, inc=1, device_id=next_id, device_id_type=MESH)

    pl.semaphore_wait(barrier, slots - 1 + has_prev.astype(jnp.int32) + has_next.astype(jnp.int32))

    def exchange(kind, source, target, head):
        for step in range(1, slots):
            peer = (slot + step) % slots
            pltpu.make_async_remote_copy(
                src_ref=source.at[:, columns(peer, head)],
                dst_ref=target.at[head, own_rows, :],
                send_sem=in_send.at[kind],
                recv_sem=in_recv.at[kind, head],
                device_id=device_of(peer),
                device_id_type=MESH,
            ).start()
        pltpu.make_async_copy(
            source.at[:, columns(slot, head)], target.at[head, own_rows, :], in_recv.at[kind, head]
        ).start()

    for head in range(heads):
        exchange(0, q_ref, q_buf, head)
    for head in range(heads):
        exchange(1, k_ref, k_buf, head)
        exchange(2, v_ref, v_buf, head)

    for copy in small:
        copy.wait()

    position = plane * DOC_MAX + lax.broadcasted_iota(jnp.int32, (1, 2 * DOC_MAX), 1)

    def next_document(index, carry):
        end, start = carry
        end = end + doc_ref[index]
        return end, jnp.where(position >= end, end, start)

    start = lax.fori_loop(
        0, doc_ref.shape[0], next_document, (jnp.int32(0), jnp.zeros((1, 2 * DOC_MAX), jnp.int32))
    )[1]
    start_buf[...] = (start - plane * DOC_MAX).astype(jnp.float32)
    pos_buf[...] = lax.broadcasted_iota(jnp.int32, (DOC_MAX, BLOCK), 0).astype(jnp.float32)

    def whole(ref, sem):
        return pltpu.make_async_copy(ref, ref, sem)

    def z_copy(kind, head, index, source, target, device_id):
        return pltpu.make_async_remote_copy(
            src_ref=source,
            dst_ref=target,
            send_sem=z_send.at[kind, head, index],
            recv_sem=z_recv.at[kind, head, index],
            device_id=device_id,
            device_id_type=MESH,
        )

    scale = LOG2E / math.sqrt(width)
    blocks = DOC_MAX // BLOCK

    def score(head, query_first, key_first, key_count, slope, shift):
        keys = k_buf[head, pl.ds(key_first, key_count), :]
        query = q_buf[head, pl.ds(query_first, BLOCK), :]
        product = lax.dot_general(
            keys, query, (((1,), (1,)), ((), ())), preferred_element_type=jnp.float32
        )
        key_pos = pos_buf[pl.ds(key_first, key_count), :]
        allowed = key_pos >= start_buf[:, pl.ds(query_first, BLOCK)]
        return product * scale + (slope * key_pos + shift), allowed

    def weighted(key_first, key_count, weights):
        return jnp.dot(
            vt_buf[:, pl.ds(key_first, key_count)],
            weights.astype(jnp.bfloat16),
            preferred_element_type=jnp.float32,
        )

    def far(head, slope):
        for index in range(blocks):
            first, count = index * BLOCK, DOC_MAX - index * BLOCK
            scores, allowed = score(head, DOC_MAX + first, first, count, slope, -DOC_MAX * slope)
            scores = jnp.where(allowed, scores, NEG_FILL)
            row_max = jnp.max(scores, axis=0, keepdims=True)
            weights = jnp.exp2(scores - row_max)
            row_total = jnp.sum(weights, axis=0, keepdims=True)
            part = weighted(first, count, weights) / row_total
            far_out[head, index] = part.astype(far_out.dtype)
            lse_out[head, index] = row_max + jnp.log2(row_total)
            z_copy(1, head, index, far_out.at[head, index], far_in.at[head, index], next_id).start()
            z_copy(2, head, index, lse_out.at[head, index], lse_in.at[head, index], next_id).start()

    def near(head, slope):
        for index in range(blocks):
            first = index * BLOCK
            scores, allowed = score(head, first, first, BLOCK, slope, 0.0)
            causal = lax.broadcasted_iota(jnp.int32, (BLOCK, BLOCK), 0) <= (
                lax.broadcasted_iota(jnp.int32, (BLOCK, BLOCK), 1)
            )
            pieces = [(first, BLOCK, jnp.where(allowed & causal, scores, NEG_FILL))]
            if index:
                scores, allowed = score(head, first, 0, first, slope, 0.0)
                pieces.append((0, first, jnp.where(allowed, scores, NEG_FILL)))
            row_max = functools.reduce(
                jnp.maximum, [jnp.max(piece, axis=0, keepdims=True) for _, _, piece in pieces]
            )
            row_total, total = 0.0, 0.0
            for key_first, key_count, piece in pieces:
                weights = jnp.exp2(piece - row_max)
                row_total = row_total + jnp.sum(weights, axis=0, keepdims=True)
                total = total + weighted(key_first, key_count, weights)
            near_sum[:, pl.ds(first, BLOCK)] = total
            near_max[:, pl.ds(first, BLOCK)] = row_max
            near_total[:, pl.ds(first, BLOCK)] = row_total

    def send_home(head, index):
        for part in range(BLOCK // rows):
            peer = index * (BLOCK // rows) + part
            done_rows = o_buf.at[head, pl.ds(peer * rows, rows), :]

            @pl.when(peer != slot)
            def _():
                pltpu.make_async_remote_copy(
                    src_ref=done_rows,
                    dst_ref=out_ref.at[:, columns(slot, head)],
                    send_sem=out_send,
                    recv_sem=out_recv,
                    device_id=device_of(peer),
                    device_id_type=MESH,
                ).start()

            @pl.when(peer == slot)
            def _():
                pltpu.make_async_copy(
                    done_rows, out_ref.at[:, columns(slot, head)], out_recv
                ).start()

    def finish(head, send):
        for index in range(blocks):
            part = pl.ds(index * BLOCK, BLOCK)

            @pl.when(has_prev)
            def _():
                whole(far_in.at[head, index], z_recv.at[1, head, index]).wait()
                whole(lse_in.at[head, index], z_recv.at[2, head, index]).wait()
                far_lse = lse_in[head, index]
                top = jnp.maximum(near_max[:, part], far_lse)
                near_scale = jnp.exp2(near_max[:, part] - top)
                far_scale = jnp.exp2(far_lse - top)
                inverse = 1.0 / (near_total[:, part] * near_scale + far_scale)
                merged = near_sum[:, part] * (near_scale * inverse)
                merged = merged + far_in[head, index].astype(jnp.float32) * (far_scale * inverse)
                o_buf[head, part, :] = merged.T.astype(o_buf.dtype)

            @pl.when(jnp.logical_not(has_prev))
            def _():
                alone = near_sum[:, part] / near_total[:, part]
                o_buf[head, part, :] = alone.T.astype(o_buf.dtype)

            if send:
                send_home(head, index)

    def queries_back(head, unused):
        whole(q_buf.at[head, pl.ds(0, DOC_MAX), :], in_recv.at[0, head]).wait()

        @pl.when(has_prev)
        def _():
            z_copy(
                0, head, 0,
                q_buf.at[head, pl.ds(0, DOC_MAX), :],
                q_buf.at[head, pl.ds(DOC_MAX, DOC_MAX), :],
                prev_id,
            ).start()

        return unused

    lax.fori_loop(0, heads, queries_back, 0)

    def one_head(head, unused):
        slope = slope_ref[slot * heads + head] * LOG2E
        whole(k_buf.at[head], in_recv.at[1, head]).wait()
        whole(v_buf.at[head], in_recv.at[2, head]).wait()

        @pl.when(head == heads - 1)
        def _():
            def send_early(early, unused):
                for index in range(blocks):
                    send_home(early, index)
                return unused

            lax.fori_loop(0, heads - 2, send_early, 0)

        vt_buf[...] = v_buf[head].T

        @pl.when(has_next)
        def _():
            whole(q_buf.at[head, pl.ds(DOC_MAX, DOC_MAX), :], z_recv.at[0, head, 0]).wait()
            far(head, slope)

        @pl.when(head > 0)
        def _():
            finish(head - 1, False)

        @pl.when(head == heads - 1)
        def _():
            for index in range(blocks):
                send_home(heads - 2, index)

        near(head, slope)
        return unused

    lax.fori_loop(0, heads, one_head, 0)
    finish(heads - 1, True)

    sent = pl.ds(0, (slots - 1) * heads * width)
    for kind, source in enumerate((q_ref, k_ref, v_ref)):
        whole(source.at[:, sent], in_send.at[kind]).wait()
    whole(out_ref.at[:, sent], out_send).wait()
    for head in range(heads):

        @pl.when(has_prev)
        def _():
            whole(q_buf.at[head, pl.ds(0, DOC_MAX), :], z_send.at[0, head, 0]).wait()

        @pl.when(has_next)
        def _():
            for index in range(blocks):
                whole(far_out.at[head, index], z_send.at[1, head, index]).wait()
                whole(lse_out.at[head, index], z_send.at[2, head, index]).wait()

    whole(out_ref, out_recv).wait()


def per_device(query_states, key_states, value_states, doc_lengths, slopes):
    rows, all_columns = query_states.shape
    width = all_columns // slopes.shape[0]
    inner_count = lax.axis_size("inner")
    plane_groups = DOC_MAX // (rows * inner_count)
    slots = plane_groups * inner_count
    planes = lax.axis_size("outer") // plane_groups
    heads = slopes.shape[0] // slots
    blocks = DOC_MAX // BLOCK
    dtype = query_states.dtype
    return pl.pallas_call(
        functools.partial(kernel, plane_groups, inner_count, planes, heads, width),
        out_shape=jax.ShapeDtypeStruct((rows, all_columns), dtype),
        in_specs=[pl.BlockSpec(memory_space=pltpu.HBM)] * 5,
        out_specs=pl.BlockSpec(memory_space=pltpu.HBM),
        scratch_shapes=[
            pltpu.SMEM(doc_lengths.shape, doc_lengths.dtype),
            pltpu.SMEM(slopes.shape, slopes.dtype),
            pltpu.VMEM((heads, 2 * DOC_MAX, width), dtype),
            pltpu.VMEM((heads, DOC_MAX, width), dtype),
            pltpu.VMEM((heads, DOC_MAX, width), dtype),
            pltpu.VMEM((width, DOC_MAX), dtype),
            pltpu.VMEM((heads, DOC_MAX, width), dtype),
            pltpu.VMEM((heads, blocks, width, BLOCK), dtype),
            pltpu.VMEM((heads, blocks, width, BLOCK), dtype),
            pltpu.VMEM((heads, blocks, 1, BLOCK), jnp.float32),
            pltpu.VMEM((heads, blocks, 1, BLOCK), jnp.float32),
            pltpu.VMEM((width, DOC_MAX), jnp.float32),
            pltpu.VMEM((1, DOC_MAX), jnp.float32),
            pltpu.VMEM((1, DOC_MAX), jnp.float32),
            pltpu.VMEM((1, 2 * DOC_MAX), jnp.float32),
            pltpu.VMEM((DOC_MAX, BLOCK), jnp.float32),
            pltpu.SemaphoreType.DMA((2,)),
            pltpu.SemaphoreType.DMA((3,)),
            pltpu.SemaphoreType.DMA((3, heads)),
            pltpu.SemaphoreType.DMA((3, heads, blocks)),
            pltpu.SemaphoreType.DMA((3, heads, blocks)),
            pltpu.SemaphoreType.DMA,
            pltpu.SemaphoreType.DMA,
        ],
        compiler_params=pltpu.CompilerParams(
            collective_id=0, has_side_effects=True, vmem_limit_bytes=64 * 1024 * 1024
        ),
        cost_estimate=pl.CostEstimate(
            flops=4 * heads * DOC_MAX * (DOC_MAX + BLOCK) * width,
            bytes_accessed=8 * rows * all_columns,
            transcendentals=heads * DOC_MAX * (DOC_MAX + BLOCK),
        ),
    )(doc_lengths, slopes, query_states, key_states, value_states)


def solution(mesh):
    placed = P(("outer", "inner"), None)
    return jax.shard_map(
        per_device,
        mesh=mesh,
        in_specs=(placed, placed, placed, P(), P()),
        out_specs=placed,
        check_vma=False,
    )
```

```python
import functools
import math

import jax
import jax.numpy as jnp
from jax import lax
from jax.experimental import pallas as pl
from jax.experimental.pallas import tpu as pltpu
from jax.sharding import PartitionSpec as P

DOC_MAX = 1024
BLOCK = 256
NEG_FILL = -1e30
LOG2E = math.log2(math.e)
MESH = pl.DeviceIdType.MESH


def kernel(
    plane_groups, inner_count, planes, heads, width,
    doc_hbm, slope_hbm, q_ref, k_ref, v_ref, out_ref,
    doc_ref, slope_ref, q_buf, k_buf, v_buf, vt_buf, o_buf,
    far_out, far_in, lse_out, lse_in, near_sum, near_max, near_total, far_weights, near_weights, far_inverse, start_buf, pos_buf,
    small_sem, in_send, in_recv, z_send, z_recv, out_send, out_recv,
):
    rows = q_ref.shape[0]
    slots = plane_groups * inner_count
    outer = lax.axis_index("outer")
    inner = lax.axis_index("inner")
    plane = outer // plane_groups
    slot = (outer % plane_groups) * inner_count + inner
    has_prev = plane > 0
    has_next = plane < planes - 1
    prev_id = {"outer": outer - plane_groups, "inner": inner}
    next_id = {"outer": outer + plane_groups, "inner": inner}

    def device_of(peer):
        return {"outer": plane * plane_groups + peer // inner_count, "inner": peer % inner_count}

    def partner(step):
        peer, unit = 0, 1
        while unit < slots:
            peer = peer + (slot // unit + step // unit) % 2 * unit
            unit = 2 * unit
        return peer

    peers = [partner(step) for step in sorted(range(1, slots), key=lambda step: (step % 2, step))]
    peers = peers[: slots // 2 - 1] + peers[slots // 2 :] + peers[slots // 2 - 1 : slots // 2]

    def columns(owner, head):
        return pl.ds(pl.multiple_of((owner * heads + head) * width, width), width)

    own_rows = pl.ds(pl.multiple_of(slot * rows, rows), rows)

    small = [
        pltpu.make_async_copy(doc_hbm, doc_ref, small_sem.at[0]),
        pltpu.make_async_copy(slope_hbm, slope_ref, small_sem.at[1]),
    ]
    for copy in small:
        copy.start()

    barrier = pltpu.get_barrier_semaphore()
    for peer in peers:
        pl.semaphore_signal(barrier, inc=1, device_id=device_of(peer), device_id_type=MESH)

    @pl.when(has_prev)
    def _():
        pl.semaphore_signal(barrier, inc=1, device_id=prev_id, device_id_type=MESH)

    @pl.when(has_next)
    def _():
        pl.semaphore_signal(barrier, inc=1, device_id=next_id, device_id_type=MESH)

    pl.semaphore_wait(barrier, slots - 1 + has_prev.astype(jnp.int32) + has_next.astype(jnp.int32))

    def exchange(kind, source, target, head):
        for peer in peers:
            pltpu.make_async_remote_copy(
                src_ref=source.at[:, columns(peer, head)],
                dst_ref=target.at[head, own_rows, :],
                send_sem=in_send.at[kind],
                recv_sem=in_recv.at[kind, head],
                device_id=device_of(peer),
                device_id_type=MESH,
            ).start()
        pltpu.make_async_copy(
            source.at[:, columns(slot, head)], target.at[head, own_rows, :], in_recv.at[kind, head]
        ).start()

    for head in range(heads):
        exchange(0, q_ref, q_buf, head)
    for head in range(heads):
        exchange(1, k_ref, k_buf, head)
        exchange(2, v_ref, v_buf, head)

    for copy in small:
        copy.wait()

    position = plane * DOC_MAX + lax.broadcasted_iota(jnp.int32, (1, 2 * DOC_MAX), 1)

    def next_document(index, carry):
        end, start = carry
        end = end + doc_ref[index]
        return end, jnp.where(position >= end, end, start)

    start = lax.fori_loop(
        0, doc_ref.shape[0], next_document, (jnp.int32(0), jnp.zeros((1, 2 * DOC_MAX), jnp.int32))
    )[1]
    start_buf[...] = (start - plane * DOC_MAX).astype(jnp.float32)
    pos_buf[...] = lax.broadcasted_iota(jnp.int32, (DOC_MAX, BLOCK), 0).astype(jnp.float32)

    def whole(ref, sem):
        return pltpu.make_async_copy(ref, ref, sem)

    def z_copy(kind, head, index, source, target, device_id):
        return pltpu.make_async_remote_copy(
            src_ref=source,
            dst_ref=target,
            send_sem=z_send.at[kind, head, index],
            recv_sem=z_recv.at[kind, head, index],
            device_id=device_id,
            device_id_type=MESH,
        )

    scale = LOG2E / math.sqrt(width)
    blocks = DOC_MAX // BLOCK

    def score(head, query_first, key_first, key_count, slope, shift):
        keys = k_buf[head, pl.ds(key_first, key_count), :]
        query = q_buf[head, pl.ds(query_first, BLOCK), :]
        product = lax.dot_general(
            keys, query, (((1,), (1,)), ((), ())), preferred_element_type=jnp.float32
        )
        key_pos = pos_buf[pl.ds(key_first, key_count), :]
        allowed = key_pos >= start_buf[:, pl.ds(query_first, BLOCK)]
        return product * scale + (slope * key_pos + shift), allowed

    def weighted(key_first, key_count, weights):
        return jnp.dot(
            vt_buf[:, pl.ds(key_first, key_count)], weights, preferred_element_type=jnp.float32
        )

    def far_place(index):
        return pl.ds(index * DOC_MAX - index * (index - 1) // 2 * BLOCK, DOC_MAX - index * BLOCK)

    def near_place(index):
        return index * (index + 1) // 2 * BLOCK

    def far_weigh(head, slope):
        for index in range(blocks):
            first, count = index * BLOCK, DOC_MAX - index * BLOCK
            scores, allowed = score(head, DOC_MAX + first, first, count, slope, -DOC_MAX * slope)
            scores = jnp.where(allowed, scores, NEG_FILL)
            row_max = jnp.max(scores, axis=0, keepdims=True)
            weights = jnp.exp2(scores - row_max)
            row_total = jnp.sum(weights, axis=0, keepdims=True)
            far_weights[far_place(index), :] = weights.astype(far_weights.dtype)
            far_inverse[:, pl.ds(first, BLOCK)] = 1.0 / row_total
            lse_out[head, index] = row_max + jnp.log2(row_total)

    def far_send(head):
        for index in range(blocks):
            first, count = index * BLOCK, DOC_MAX - index * BLOCK
            part = weighted(first, count, far_weights[far_place(index), :])
            part = part * far_inverse[:, pl.ds(first, BLOCK)]
            far_out[head, index] = part.astype(far_out.dtype)
            z_copy(1, head, index, far_out.at[head, index], far_in.at[head, index], next_id).start()
            z_copy(2, head, index, lse_out.at[head, index], lse_in.at[head, index], next_id).start()

    def near_weigh(head, slope):
        for index in range(blocks):
            first, place = index * BLOCK, near_place(index)
            scores, allowed = score(head, first, first, BLOCK, slope, 0.0)
            causal = lax.broadcasted_iota(jnp.int32, (BLOCK, BLOCK), 0) <= (
                lax.broadcasted_iota(jnp.int32, (BLOCK, BLOCK), 1)
            )
            pieces = [(place + first, BLOCK, jnp.where(allowed & causal, scores, NEG_FILL))]
            if index:
                scores, allowed = score(head, first, 0, first, slope, 0.0)
                pieces.append((place, first, jnp.where(allowed, scores, NEG_FILL)))
            row_max = functools.reduce(
                jnp.maximum, [jnp.max(piece, axis=0, keepdims=True) for _, _, piece in pieces]
            )
            row_total = 0.0
            for piece_first, count, piece in pieces:
                weights = jnp.exp2(piece - row_max)
                row_total = row_total + jnp.sum(weights, axis=0, keepdims=True)
                near_weights[pl.ds(piece_first, count), :] = weights.astype(near_weights.dtype)
            near_max[head, :, pl.ds(first, BLOCK)] = row_max
            near_total[head, :, pl.ds(first, BLOCK)] = row_total

    def near_add():
        for index in range(blocks):
            count = (index + 1) * BLOCK
            weights = near_weights[pl.ds(near_place(index), count), :]
            near_sum[:, pl.ds(index * BLOCK, BLOCK)] = weighted(0, count, weights)

    def send_home(head, index):
        for part in range(BLOCK // rows):
            peer = index * (BLOCK // rows) + part
            done_rows = o_buf.at[head, pl.ds(peer * rows, rows), :]

            @pl.when(peer != slot)
            def _():
                pltpu.make_async_remote_copy(
                    src_ref=done_rows,
                    dst_ref=out_ref.at[:, columns(slot, head)],
                    send_sem=out_send,
                    recv_sem=out_recv,
                    device_id=device_of(peer),
                    device_id_type=MESH,
                ).start()

            @pl.when(peer == slot)
            def _():
                pltpu.make_async_copy(
                    done_rows, out_ref.at[:, columns(slot, head)], out_recv
                ).start()

    def finish(head):
        for index in range(blocks):
            part = pl.ds(index * BLOCK, BLOCK)

            @pl.when(has_prev)
            def _():
                whole(far_in.at[head, index], z_recv.at[1, head, index]).wait()
                whole(lse_in.at[head, index], z_recv.at[2, head, index]).wait()
                far_lse = lse_in[head, index]
                top = jnp.maximum(near_max[head, :, part], far_lse)
                near_scale = jnp.exp2(near_max[head, :, part] - top)
                far_scale = jnp.exp2(far_lse - top)
                inverse = 1.0 / (near_total[head, :, part] * near_scale + far_scale)
                merged = near_sum[:, part] * (near_scale * inverse)
                merged = merged + far_in[head, index].astype(jnp.float32) * (far_scale * inverse)
                o_buf[head, part, :] = merged.T.astype(o_buf.dtype)

            @pl.when(jnp.logical_not(has_prev))
            def _():
                alone = near_sum[:, part] / near_total[head, :, part]
                o_buf[head, part, :] = alone.T.astype(o_buf.dtype)

            send_home(head, index)

    def queries_back(head, unused):
        whole(q_buf.at[head, pl.ds(0, DOC_MAX), :], in_recv.at[0, head]).wait()

        @pl.when(has_prev)
        def _():
            z_copy(
                0, head, 0,
                q_buf.at[head, pl.ds(0, DOC_MAX), :],
                q_buf.at[head, pl.ds(DOC_MAX, DOC_MAX), :],
                prev_id,
            ).start()

        return unused

    lax.fori_loop(0, heads, queries_back, 0)

    def one_head(head, unused):
        slope = slope_ref[slot * heads + head] * LOG2E
        whole(k_buf.at[head], in_recv.at[1, head]).wait()

        @pl.when(has_next)
        def _():
            whole(q_buf.at[head, pl.ds(DOC_MAX, DOC_MAX), :], z_recv.at[0, head, 0]).wait()
            far_weigh(head, slope)

        near_weigh(head, slope)
        whole(v_buf.at[head], in_recv.at[2, head]).wait()
        vt_buf[...] = v_buf[head].T

        @pl.when(has_next)
        def _():
            far_send(head)

        @pl.when(head > 0)
        def _():
            finish(head - 1)

        near_add()
        return unused

    lax.fori_loop(0, heads, one_head, 0)
    finish(heads - 1)

    sent = pl.ds(0, (slots - 1) * heads * width)
    for kind, source in enumerate((q_ref, k_ref, v_ref)):
        whole(source.at[:, sent], in_send.at[kind]).wait()
    whole(out_ref.at[:, sent], out_send).wait()
    for head in range(heads):

        @pl.when(has_prev)
        def _():
            whole(q_buf.at[head, pl.ds(0, DOC_MAX), :], z_send.at[0, head, 0]).wait()

        @pl.when(has_next)
        def _():
            for index in range(blocks):
                whole(far_out.at[head, index], z_send.at[1, head, index]).wait()
                whole(lse_out.at[head, index], z_send.at[2, head, index]).wait()

    whole(out_ref, out_recv).wait()


def per_device(query_states, key_states, value_states, doc_lengths, slopes):
    rows, all_columns = query_states.shape
    width = all_columns // slopes.shape[0]
    inner_count = lax.axis_size("inner")
    plane_groups = DOC_MAX // (rows * inner_count)
    slots = plane_groups * inner_count
    planes = lax.axis_size("outer") // plane_groups
    heads = slopes.shape[0] // slots
    blocks = DOC_MAX // BLOCK
    dtype = query_states.dtype
    return pl.pallas_call(
        functools.partial(kernel, plane_groups, inner_count, planes, heads, width),
        out_shape=jax.ShapeDtypeStruct((rows, all_columns), dtype),
        in_specs=[pl.BlockSpec(memory_space=pltpu.HBM)] * 5,
        out_specs=pl.BlockSpec(memory_space=pltpu.HBM),
        scratch_shapes=[
            pltpu.SMEM(doc_lengths.shape, doc_lengths.dtype),
            pltpu.SMEM(slopes.shape, slopes.dtype),
            pltpu.VMEM((heads, 2 * DOC_MAX, width), dtype),
            pltpu.VMEM((heads, DOC_MAX, width), dtype),
            pltpu.VMEM((heads, DOC_MAX, width), dtype),
            pltpu.VMEM((width, DOC_MAX), dtype),
            pltpu.VMEM((heads, DOC_MAX, width), dtype),
            pltpu.VMEM((heads, blocks, width, BLOCK), dtype),
            pltpu.VMEM((heads, blocks, width, BLOCK), dtype),
            pltpu.VMEM((heads, blocks, 1, BLOCK), jnp.float32),
            pltpu.VMEM((heads, blocks, 1, BLOCK), jnp.float32),
            pltpu.VMEM((width, DOC_MAX), jnp.float32),
            pltpu.VMEM((heads, 1, DOC_MAX), jnp.float32),
            pltpu.VMEM((heads, 1, DOC_MAX), jnp.float32),
            pltpu.VMEM((blocks * (blocks + 1) // 2 * BLOCK, BLOCK), dtype),
            pltpu.VMEM((blocks * (blocks + 1) // 2 * BLOCK, BLOCK), dtype),
            pltpu.VMEM((1, DOC_MAX), jnp.float32),
            pltpu.VMEM((1, 2 * DOC_MAX), jnp.float32),
            pltpu.VMEM((DOC_MAX, BLOCK), jnp.float32),
            pltpu.SemaphoreType.DMA((2,)),
            pltpu.SemaphoreType.DMA((3,)),
            pltpu.SemaphoreType.DMA((3, heads)),
            pltpu.SemaphoreType.DMA((3, heads, blocks)),
            pltpu.SemaphoreType.DMA((3, heads, blocks)),
            pltpu.SemaphoreType.DMA,
            pltpu.SemaphoreType.DMA,
        ],
        compiler_params=pltpu.CompilerParams(
            collective_id=0, has_side_effects=True, vmem_limit_bytes=64 * 1024 * 1024
        ),
        cost_estimate=pl.CostEstimate(
            flops=4 * heads * DOC_MAX * (DOC_MAX + BLOCK) * width,
            bytes_accessed=8 * rows * all_columns,
            transcendentals=heads * DOC_MAX * (DOC_MAX + BLOCK),
        ),
    )(doc_lengths, slopes, query_states, key_states, value_states)


def solution(mesh):
    placed = P(("outer", "inner"), None)
    return jax.shard_map(
        per_device,
        mesh=mesh,
        in_specs=(placed, placed, placed, P(), P()),
        out_specs=placed,
        check_vma=False,
    )
```

```python
import functools
import math

import jax
import jax.numpy as jnp
from jax import lax
from jax.experimental import pallas as pl
from jax.experimental.pallas import tpu as pltpu
from jax.sharding import PartitionSpec as P

DOC_MAX = 1024
BLOCK = 256
NEG_FILL = -1e30
LOG2E = math.log2(math.e)
MESH = pl.DeviceIdType.MESH


def kernel(
    plane_groups, inner_count, planes, heads, width,
    doc_hbm, slope_hbm, q_ref, k_ref, v_ref, out_ref,
    doc_ref, slope_ref, q_buf, k_buf, v_buf, vt_buf, o_buf,
    far_out, far_in, lse_out, lse_in, near_sum, near_max, near_total, far_weights, near_weights, far_inverse, start_buf, pos_buf,
    small_sem, in_send, in_recv, z_send, z_recv, out_send, out_recv,
):
    rows = q_ref.shape[0]
    slots = plane_groups * inner_count
    outer = lax.axis_index("outer")
    inner = lax.axis_index("inner")
    plane = outer // plane_groups
    slot = (outer % plane_groups) * inner_count + inner
    has_prev = plane > 0
    has_next = plane < planes - 1
    prev_id = {"outer": outer - plane_groups, "inner": inner}
    next_id = {"outer": outer + plane_groups, "inner": inner}

    def device_of(peer):
        return {"outer": plane * plane_groups + peer // inner_count, "inner": peer % inner_count}

    peers = [(slot + step) % slots for step in range(1, slots)]

    def columns(owner, head):
        return pl.ds(pl.multiple_of((owner * heads + head) * width, width), width)

    own_rows = pl.ds(pl.multiple_of(slot * rows, rows), rows)

    small = [
        pltpu.make_async_copy(doc_hbm, doc_ref, small_sem.at[0]),
        pltpu.make_async_copy(slope_hbm, slope_ref, small_sem.at[1]),
    ]
    for copy in small:
        copy.start()

    barrier = pltpu.get_barrier_semaphore()
    for peer in peers:
        pl.semaphore_signal(barrier, inc=1, device_id=device_of(peer), device_id_type=MESH)

    @pl.when(has_prev)
    def _():
        pl.semaphore_signal(barrier, inc=1, device_id=prev_id, device_id_type=MESH)

    @pl.when(has_next)
    def _():
        pl.semaphore_signal(barrier, inc=1, device_id=next_id, device_id_type=MESH)

    pl.semaphore_wait(barrier, slots - 1 + has_prev.astype(jnp.int32) + has_next.astype(jnp.int32))

    def exchange(kind, source, target, head):
        for peer in peers:
            pltpu.make_async_remote_copy(
                src_ref=source.at[:, columns(peer, head)],
                dst_ref=target.at[head, own_rows, :],
                send_sem=in_send.at[kind],
                recv_sem=in_recv.at[kind, head],
                device_id=device_of(peer),
                device_id_type=MESH,
            ).start()
        pltpu.make_async_copy(
            source.at[:, columns(slot, head)], target.at[head, own_rows, :], in_recv.at[kind, head]
        ).start()

    for head in range(heads):
        exchange(0, q_ref, q_buf, head)
    for head in range(heads):
        exchange(1, k_ref, k_buf, head)
        exchange(2, v_ref, v_buf, head)

    for copy in small:
        copy.wait()

    position = plane * DOC_MAX + lax.broadcasted_iota(jnp.int32, (1, 2 * DOC_MAX), 1)

    def next_document(index, carry):
        end, start = carry
        end = end + doc_ref[index]
        return end, jnp.where(position >= end, end, start)

    start = lax.fori_loop(
        0, doc_ref.shape[0], next_document, (jnp.int32(0), jnp.zeros((1, 2 * DOC_MAX), jnp.int32))
    )[1]
    start_buf[...] = (start - plane * DOC_MAX).astype(jnp.float32)
    pos_buf[...] = lax.broadcasted_iota(jnp.int32, (DOC_MAX, BLOCK), 0).astype(jnp.float32)

    def whole(ref, sem):
        return pltpu.make_async_copy(ref, ref, sem)

    def z_copy(kind, head, index, source, target, device_id):
        return pltpu.make_async_remote_copy(
            src_ref=source,
            dst_ref=target,
            send_sem=z_send.at[kind, head, index],
            recv_sem=z_recv.at[kind, head, index],
            device_id=device_id,
            device_id_type=MESH,
        )

    scale = LOG2E / math.sqrt(width)
    blocks = DOC_MAX // BLOCK

    def score(head, query_first, key_first, key_count, slope, shift):
        keys = k_buf[head, pl.ds(key_first, key_count), :]
        query = q_buf[head, pl.ds(query_first, BLOCK), :]
        product = lax.dot_general(
            keys, query, (((1,), (1,)), ((), ())), preferred_element_type=jnp.float32
        )
        key_pos = pos_buf[pl.ds(key_first, key_count), :]
        allowed = key_pos >= start_buf[:, pl.ds(query_first, BLOCK)]
        return product * scale + (slope * key_pos + shift), allowed

    def weighted(key_first, key_count, weights):
        return jnp.dot(
            vt_buf[:, pl.ds(key_first, key_count)], weights, preferred_element_type=jnp.float32
        )

    def far_place(index):
        return pl.ds(index * DOC_MAX - index * (index - 1) // 2 * BLOCK, DOC_MAX - index * BLOCK)

    def near_place(index):
        return index * (index + 1) // 2 * BLOCK

    def far_weigh(head, slope):
        for index in range(blocks):
            first, count = index * BLOCK, DOC_MAX - index * BLOCK
            scores, allowed = score(head, DOC_MAX + first, first, count, slope, -DOC_MAX * slope)
            scores = jnp.where(allowed, scores, NEG_FILL)
            row_max = jnp.max(scores, axis=0, keepdims=True)
            weights = jnp.exp2(scores - row_max)
            row_total = jnp.sum(weights, axis=0, keepdims=True)
            far_weights[far_place(index), :] = weights.astype(far_weights.dtype)
            far_inverse[:, pl.ds(first, BLOCK)] = 1.0 / row_total
            lse_out[head, index] = row_max + jnp.log2(row_total)

    def far_send(head):
        for index in range(blocks):
            first, count = index * BLOCK, DOC_MAX - index * BLOCK
            part = weighted(first, count, far_weights[far_place(index), :])
            part = part * far_inverse[:, pl.ds(first, BLOCK)]
            far_out[head, index] = part.astype(far_out.dtype)
            z_copy(1, head, index, far_out.at[head, index], far_in.at[head, index], next_id).start()
            z_copy(2, head, index, lse_out.at[head, index], lse_in.at[head, index], next_id).start()

    def near_weigh(head, slope):
        for index in range(blocks):
            first, place = index * BLOCK, near_place(index)
            scores, allowed = score(head, first, first, BLOCK, slope, 0.0)
            causal = lax.broadcasted_iota(jnp.int32, (BLOCK, BLOCK), 0) <= (
                lax.broadcasted_iota(jnp.int32, (BLOCK, BLOCK), 1)
            )
            pieces = [(place + first, BLOCK, jnp.where(allowed & causal, scores, NEG_FILL))]
            if index:
                scores, allowed = score(head, first, 0, first, slope, 0.0)
                pieces.append((place, first, jnp.where(allowed, scores, NEG_FILL)))
            row_max = functools.reduce(
                jnp.maximum, [jnp.max(piece, axis=0, keepdims=True) for _, _, piece in pieces]
            )
            row_total = 0.0
            for piece_first, count, piece in pieces:
                weights = jnp.exp2(piece - row_max)
                row_total = row_total + jnp.sum(weights, axis=0, keepdims=True)
                near_weights[pl.ds(piece_first, count), :] = weights.astype(near_weights.dtype)
            near_max[head, :, pl.ds(first, BLOCK)] = row_max
            near_total[head, :, pl.ds(first, BLOCK)] = row_total

    def near_add():
        for index in range(blocks):
            count = (index + 1) * BLOCK
            weights = near_weights[pl.ds(near_place(index), count), :]
            near_sum[:, pl.ds(index * BLOCK, BLOCK)] = weighted(0, count, weights)

    def send_home(head, index):
        for part in range(BLOCK // rows):
            peer = index * (BLOCK // rows) + part
            done_rows = o_buf.at[head, pl.ds(peer * rows, rows), :]

            @pl.when(peer != slot)
            def _():
                pltpu.make_async_remote_copy(
                    src_ref=done_rows,
                    dst_ref=out_ref.at[:, columns(slot, head)],
                    send_sem=out_send,
                    recv_sem=out_recv,
                    device_id=device_of(peer),
                    device_id_type=MESH,
                ).start()

            @pl.when(peer == slot)
            def _():
                pltpu.make_async_copy(
                    done_rows, out_ref.at[:, columns(slot, head)], out_recv
                ).start()

    def finish(head):
        for index in range(blocks):
            part = pl.ds(index * BLOCK, BLOCK)

            @pl.when(has_prev)
            def _():
                whole(far_in.at[head, index], z_recv.at[1, head, index]).wait()
                whole(lse_in.at[head, index], z_recv.at[2, head, index]).wait()
                far_lse = lse_in[head, index]
                top = jnp.maximum(near_max[head, :, part], far_lse)
                near_scale = jnp.exp2(near_max[head, :, part] - top)
                far_scale = jnp.exp2(far_lse - top)
                inverse = 1.0 / (near_total[head, :, part] * near_scale + far_scale)
                merged = near_sum[:, part] * (near_scale * inverse)
                merged = merged + far_in[head, index].astype(jnp.float32) * (far_scale * inverse)
                o_buf[head, part, :] = merged.T.astype(o_buf.dtype)

            @pl.when(jnp.logical_not(has_prev))
            def _():
                alone = near_sum[:, part] / near_total[head, :, part]
                o_buf[head, part, :] = alone.T.astype(o_buf.dtype)

            send_home(head, index)

    def queries_back(head, unused):
        whole(q_buf.at[head, pl.ds(0, DOC_MAX), :], in_recv.at[0, head]).wait()

        @pl.when(has_prev)
        def _():
            z_copy(
                0, head, 0,
                q_buf.at[head, pl.ds(0, DOC_MAX), :],
                q_buf.at[head, pl.ds(DOC_MAX, DOC_MAX), :],
                prev_id,
            ).start()

        return unused

    lax.fori_loop(0, heads, queries_back, 0)

    def one_head(head, unused):
        slope = slope_ref[slot * heads + head] * LOG2E
        whole(k_buf.at[head], in_recv.at[1, head]).wait()

        @pl.when(has_next)
        def _():
            whole(q_buf.at[head, pl.ds(DOC_MAX, DOC_MAX), :], z_recv.at[0, head, 0]).wait()
            far_weigh(head, slope)

        near_weigh(head, slope)
        whole(v_buf.at[head], in_recv.at[2, head]).wait()
        vt_buf[...] = v_buf[head].T

        @pl.when(has_next)
        def _():
            far_send(head)

        @pl.when(head > 0)
        def _():
            finish(head - 1)

        near_add()
        return unused

    lax.fori_loop(0, heads, one_head, 0)
    finish(heads - 1)

    sent = pl.ds(0, (slots - 1) * heads * width)
    for kind, source in enumerate((q_ref, k_ref, v_ref)):
        whole(source.at[:, sent], in_send.at[kind]).wait()
    whole(out_ref.at[:, sent], out_send).wait()
    for head in range(heads):

        @pl.when(has_prev)
        def _():
            whole(q_buf.at[head, pl.ds(0, DOC_MAX), :], z_send.at[0, head, 0]).wait()

        @pl.when(has_next)
        def _():
            for index in range(blocks):
                whole(far_out.at[head, index], z_send.at[1, head, index]).wait()
                whole(lse_out.at[head, index], z_send.at[2, head, index]).wait()

    whole(out_ref, out_recv).wait()


def settle(source, target, sems):
    pieces = sems.shape[0]
    rows = source.shape[0] // pieces
    copies = []
    for piece in range(pieces):
        place = pl.ds(piece * rows, rows)
        copies.append(pltpu.make_async_copy(source.at[place, :], target.at[place, :], sems.at[piece]))
    for copy in copies:
        copy.start()
    for copy in copies:
        copy.wait()


def per_device(query_states, key_states, value_states, doc_lengths, slopes):
    rows, all_columns = query_states.shape
    width = all_columns // slopes.shape[0]
    inner_count = lax.axis_size("inner")
    plane_groups = DOC_MAX // (rows * inner_count)
    slots = plane_groups * inner_count
    planes = lax.axis_size("outer") // plane_groups
    heads = slopes.shape[0] // slots
    blocks = DOC_MAX // BLOCK
    dtype = query_states.dtype
    gathered = pl.pallas_call(
        functools.partial(kernel, plane_groups, inner_count, planes, heads, width),
        out_shape=jax.ShapeDtypeStruct((rows, all_columns), dtype),
        in_specs=[pl.BlockSpec(memory_space=pltpu.HBM)] * 5,
        out_specs=pl.BlockSpec(memory_space=pltpu.HBM),
        scratch_shapes=[
            pltpu.SMEM(doc_lengths.shape, doc_lengths.dtype),
            pltpu.SMEM(slopes.shape, slopes.dtype),
            pltpu.VMEM((heads, 2 * DOC_MAX, width), dtype),
            pltpu.VMEM((heads, DOC_MAX, width), dtype),
            pltpu.VMEM((heads, DOC_MAX, width), dtype),
            pltpu.VMEM((width, DOC_MAX), dtype),
            pltpu.VMEM((heads, DOC_MAX, width), dtype),
            pltpu.VMEM((heads, blocks, width, BLOCK), dtype),
            pltpu.VMEM((heads, blocks, width, BLOCK), dtype),
            pltpu.VMEM((heads, blocks, 1, BLOCK), jnp.float32),
            pltpu.VMEM((heads, blocks, 1, BLOCK), jnp.float32),
            pltpu.VMEM((width, DOC_MAX), jnp.float32),
            pltpu.VMEM((heads, 1, DOC_MAX), jnp.float32),
            pltpu.VMEM((heads, 1, DOC_MAX), jnp.float32),
            pltpu.VMEM((blocks * (blocks + 1) // 2 * BLOCK, BLOCK), dtype),
            pltpu.VMEM((blocks * (blocks + 1) // 2 * BLOCK, BLOCK), dtype),
            pltpu.VMEM((1, DOC_MAX), jnp.float32),
            pltpu.VMEM((1, 2 * DOC_MAX), jnp.float32),
            pltpu.VMEM((DOC_MAX, BLOCK), jnp.float32),
            pltpu.SemaphoreType.DMA((2,)),
            pltpu.SemaphoreType.DMA((3,)),
            pltpu.SemaphoreType.DMA((3, heads)),
            pltpu.SemaphoreType.DMA((3, heads, blocks)),
            pltpu.SemaphoreType.DMA((3, heads, blocks)),
            pltpu.SemaphoreType.DMA,
            pltpu.SemaphoreType.DMA,
        ],
        compiler_params=pltpu.CompilerParams(
            collective_id=0, has_side_effects=True, vmem_limit_bytes=64 * 1024 * 1024
        ),
        cost_estimate=pl.CostEstimate(
            flops=4 * heads * DOC_MAX * (DOC_MAX + BLOCK) * width,
            bytes_accessed=8 * rows * all_columns,
            transcendentals=heads * DOC_MAX * (DOC_MAX + BLOCK),
        ),
    )(doc_lengths, slopes, query_states, key_states, value_states)
    return pl.pallas_call(
        settle,
        out_shape=jax.ShapeDtypeStruct((rows, all_columns), dtype),
        in_specs=[pl.BlockSpec(memory_space=pl.ANY)],
        out_specs=pl.BlockSpec(memory_space=pl.ANY),
        scratch_shapes=[pltpu.SemaphoreType.DMA((8,))],
        compiler_params=pltpu.CompilerParams(vmem_limit_bytes=64 * 1024 * 1024),
    )(gathered)


def solution(mesh):
    placed = P(("outer", "inner"), None)
    return jax.shard_map(
        per_device,
        mesh=mesh,
        in_specs=(placed, placed, placed, P(), P()),
        out_specs=placed,
        check_vma=False,
    )
```

```python
import functools
import math

import jax
import jax.numpy as jnp
from jax import lax
from jax.experimental import pallas as pl
from jax.experimental.pallas import tpu as pltpu
from jax.sharding import PartitionSpec as P

DOC_MAX = 1024
BLOCK = 256
NEG_FILL = -1e30
LOG2E = math.log2(math.e)
MESH = pl.DeviceIdType.MESH


def kernel(
    plane_groups, inner_count, planes, heads, width,
    doc_hbm, slope_hbm, q_ref, k_ref, v_ref, out_ref,
    doc_ref, slope_ref, q_buf, k_buf, v_buf, vt_buf, o_buf,
    far_out, far_in, lse_out, lse_in, near_sum, near_max, near_total, far_weights, near_weights, far_inverse, start_buf, pos_buf,
    small_sem, in_send, in_recv, z_send, z_recv, out_send, out_recv,
):
    rows = q_ref.shape[0]
    slots = plane_groups * inner_count
    outer = lax.axis_index("outer")
    inner = lax.axis_index("inner")
    plane = outer // plane_groups
    slot = (outer % plane_groups) * inner_count + inner
    has_prev = plane > 0
    has_next = plane < planes - 1
    prev_id = {"outer": outer - plane_groups, "inner": inner}
    next_id = {"outer": outer + plane_groups, "inner": inner}

    def device_of(peer):
        return {"outer": plane * plane_groups + peer // inner_count, "inner": peer % inner_count}

    peers = [(slot + step) % slots for step in range(1, slots)]

    def columns(owner, head):
        return pl.ds(pl.multiple_of((owner * heads + head) * width, width), width)

    own_rows = pl.ds(pl.multiple_of(slot * rows, rows), rows)

    small = [
        pltpu.make_async_copy(doc_hbm, doc_ref, small_sem.at[0]),
        pltpu.make_async_copy(slope_hbm, slope_ref, small_sem.at[1]),
    ]
    for copy in small:
        copy.start()

    barrier = pltpu.get_barrier_semaphore()
    for peer in peers:
        pl.semaphore_signal(barrier, inc=1, device_id=device_of(peer), device_id_type=MESH)

    @pl.when(has_prev)
    def _():
        pl.semaphore_signal(barrier, inc=1, device_id=prev_id, device_id_type=MESH)

    @pl.when(has_next)
    def _():
        pl.semaphore_signal(barrier, inc=1, device_id=next_id, device_id_type=MESH)

    pl.semaphore_wait(barrier, slots - 1 + has_prev.astype(jnp.int32) + has_next.astype(jnp.int32))

    def exchange(kind, source, target, head):
        for peer in peers:
            pltpu.make_async_remote_copy(
                src_ref=source.at[:, columns(peer, head)],
                dst_ref=target.at[head, own_rows, :],
                send_sem=in_send.at[kind],
                recv_sem=in_recv.at[kind, head],
                device_id=device_of(peer),
                device_id_type=MESH,
            ).start()
        pltpu.make_async_copy(
            source.at[:, columns(slot, head)], target.at[head, own_rows, :], in_recv.at[kind, head]
        ).start()

    def share(owner):
        return pl.ds(pl.multiple_of(owner * heads * width, heads * width), heads * width)

    for peer in peers:
        pltpu.make_async_remote_copy(
            src_ref=q_ref.at[:, share(peer)],
            dst_ref=q_buf.at[own_rows, :],
            send_sem=in_send.at[0],
            recv_sem=in_recv.at[0, 0],
            device_id=device_of(peer),
            device_id_type=MESH,
        ).start()
    pltpu.make_async_copy(q_ref.at[:, share(slot)], q_buf.at[own_rows, :], in_recv.at[0, 0]).start()
    for head in range(heads):
        exchange(1, k_ref, k_buf, head)
        exchange(2, v_ref, v_buf, head)

    for copy in small:
        copy.wait()

    position = plane * DOC_MAX + lax.broadcasted_iota(jnp.int32, (1, 2 * DOC_MAX), 1)

    def next_document(index, carry):
        end, start = carry
        end = end + doc_ref[index]
        return end, jnp.where(position >= end, end, start)

    start = lax.fori_loop(
        0, doc_ref.shape[0], next_document, (jnp.int32(0), jnp.zeros((1, 2 * DOC_MAX), jnp.int32))
    )[1]
    start_buf[...] = (start - plane * DOC_MAX).astype(jnp.float32)
    pos_buf[...] = lax.broadcasted_iota(jnp.int32, (DOC_MAX, BLOCK), 0).astype(jnp.float32)

    def whole(ref, sem):
        return pltpu.make_async_copy(ref, ref, sem)

    def z_copy(kind, head, index, source, target, device_id):
        return pltpu.make_async_remote_copy(
            src_ref=source,
            dst_ref=target,
            send_sem=z_send.at[kind, head, index],
            recv_sem=z_recv.at[kind, head, index],
            device_id=device_id,
            device_id_type=MESH,
        )

    def part_of(head):
        return pl.ds(pl.multiple_of(head * width, width), width)

    scale = LOG2E / math.sqrt(width)
    blocks = DOC_MAX // BLOCK

    def score(head, query_first, key_first, key_count, slope, shift):
        keys = k_buf[head, pl.ds(key_first, key_count), :]
        query = q_buf[pl.ds(query_first, BLOCK), part_of(head)]
        product = lax.dot_general(
            keys, query, (((1,), (1,)), ((), ())), preferred_element_type=jnp.float32
        )
        key_pos = pos_buf[pl.ds(key_first, key_count), :]
        allowed = key_pos >= start_buf[:, pl.ds(query_first, BLOCK)]
        return product * scale + (slope * key_pos + shift), allowed

    def weighted(key_first, key_count, weights):
        return jnp.dot(
            vt_buf[:, pl.ds(key_first, key_count)], weights, preferred_element_type=jnp.float32
        )

    def far_place(index):
        return pl.ds(index * DOC_MAX - index * (index - 1) // 2 * BLOCK, DOC_MAX - index * BLOCK)

    def near_place(index):
        return index * (index + 1) // 2 * BLOCK

    def far_weigh(head, slope):
        for index in range(blocks):
            first, count = index * BLOCK, DOC_MAX - index * BLOCK
            scores, allowed = score(head, DOC_MAX + first, first, count, slope, -DOC_MAX * slope)
            scores = jnp.where(allowed, scores, NEG_FILL)
            row_max = jnp.max(scores, axis=0, keepdims=True)
            weights = jnp.exp2(scores - row_max)
            row_total = jnp.sum(weights, axis=0, keepdims=True)
            far_weights[far_place(index), :] = weights.astype(far_weights.dtype)
            far_inverse[:, pl.ds(first, BLOCK)] = 1.0 / row_total
            lse_out[head, index] = row_max + jnp.log2(row_total)

    def far_send(head):
        for index in range(blocks):
            first, count = index * BLOCK, DOC_MAX - index * BLOCK
            part = weighted(first, count, far_weights[far_place(index), :])
            part = part * far_inverse[:, pl.ds(first, BLOCK)]
            far_out[head, index] = part.astype(far_out.dtype)
            z_copy(1, head, index, far_out.at[head, index], far_in.at[head, index], next_id).start()
            z_copy(2, head, index, lse_out.at[head, index], lse_in.at[head, index], next_id).start()

    def near_weigh(head, slope):
        for index in range(blocks):
            first, place = index * BLOCK, near_place(index)
            scores, allowed = score(head, first, first, BLOCK, slope, 0.0)
            causal = lax.broadcasted_iota(jnp.int32, (BLOCK, BLOCK), 0) <= (
                lax.broadcasted_iota(jnp.int32, (BLOCK, BLOCK), 1)
            )
            pieces = [(place + first, BLOCK, jnp.where(allowed & causal, scores, NEG_FILL))]
            if index:
                scores, allowed = score(head, first, 0, first, slope, 0.0)
                pieces.append((place, first, jnp.where(allowed, scores, NEG_FILL)))
            row_max = functools.reduce(
                jnp.maximum, [jnp.max(piece, axis=0, keepdims=True) for _, _, piece in pieces]
            )
            row_total = 0.0
            for piece_first, count, piece in pieces:
                weights = jnp.exp2(piece - row_max)
                row_total = row_total + jnp.sum(weights, axis=0, keepdims=True)
                near_weights[pl.ds(piece_first, count), :] = weights.astype(near_weights.dtype)
            near_max[head, :, pl.ds(first, BLOCK)] = row_max
            near_total[head, :, pl.ds(first, BLOCK)] = row_total

    def near_add():
        for index in range(blocks):
            count = (index + 1) * BLOCK
            weights = near_weights[pl.ds(near_place(index), count), :]
            near_sum[:, pl.ds(index * BLOCK, BLOCK)] = weighted(0, count, weights)

    def send_home(head, index):
        for part in range(BLOCK // rows):
            peer = index * (BLOCK // rows) + part
            done_rows = o_buf.at[head, pl.ds(peer * rows, rows), :]

            @pl.when(peer != slot)
            def _():
                pltpu.make_async_remote_copy(
                    src_ref=done_rows,
                    dst_ref=out_ref.at[:, columns(slot, head)],
                    send_sem=out_send,
                    recv_sem=out_recv,
                    device_id=device_of(peer),
                    device_id_type=MESH,
                ).start()

            @pl.when(peer == slot)
            def _():
                pltpu.make_async_copy(
                    done_rows, out_ref.at[:, columns(slot, head)], out_recv
                ).start()

    def finish(head):
        for index in range(blocks):
            part = pl.ds(index * BLOCK, BLOCK)

            @pl.when(has_prev)
            def _():
                whole(far_in.at[head, index], z_recv.at[1, head, index]).wait()
                whole(lse_in.at[head, index], z_recv.at[2, head, index]).wait()
                far_lse = lse_in[head, index]
                top = jnp.maximum(near_max[head, :, part], far_lse)
                near_scale = jnp.exp2(near_max[head, :, part] - top)
                far_scale = jnp.exp2(far_lse - top)
                inverse = 1.0 / (near_total[head, :, part] * near_scale + far_scale)
                merged = near_sum[:, part] * (near_scale * inverse)
                merged = merged + far_in[head, index].astype(jnp.float32) * (far_scale * inverse)
                o_buf[head, part, :] = merged.T.astype(o_buf.dtype)

            @pl.when(jnp.logical_not(has_prev))
            def _():
                alone = near_sum[:, part] / near_total[head, :, part]
                o_buf[head, part, :] = alone.T.astype(o_buf.dtype)

            send_home(head, index)

    whole(q_buf.at[pl.ds(0, DOC_MAX), :], in_recv.at[0, 0]).wait()

    @pl.when(has_prev)
    def _():
        for head in range(heads):
            z_copy(
                0, head, 0,
                q_buf.at[pl.ds(0, DOC_MAX), part_of(head)],
                q_buf.at[pl.ds(DOC_MAX, DOC_MAX), part_of(head)],
                prev_id,
            ).start()

    def one_head(head, unused):
        slope = slope_ref[slot * heads + head] * LOG2E
        whole(k_buf.at[head], in_recv.at[1, head]).wait()

        @pl.when(has_next)
        def _():
            whole(q_buf.at[pl.ds(DOC_MAX, DOC_MAX), part_of(head)], z_recv.at[0, head, 0]).wait()
            far_weigh(head, slope)

        near_weigh(head, slope)
        whole(v_buf.at[head], in_recv.at[2, head]).wait()
        vt_buf[...] = v_buf[head].T

        @pl.when(has_next)
        def _():
            far_send(head)

        @pl.when(head > 0)
        def _():
            finish(head - 1)

        near_add()
        return unused

    lax.fori_loop(0, heads, one_head, 0)
    finish(heads - 1)

    sent = pl.ds(0, (slots - 1) * heads * width)
    for kind, source in enumerate((q_ref, k_ref, v_ref)):
        whole(source.at[:, sent], in_send.at[kind]).wait()
    whole(out_ref.at[:, sent], out_send).wait()
    for head in range(heads):

        @pl.when(has_prev)
        def _():
            whole(q_buf.at[pl.ds(0, DOC_MAX), part_of(head)], z_send.at[0, head, 0]).wait()

        @pl.when(has_next)
        def _():
            for index in range(blocks):
                whole(far_out.at[head, index], z_send.at[1, head, index]).wait()
                whole(lse_out.at[head, index], z_send.at[2, head, index]).wait()

    whole(out_ref, out_recv).wait()


def settle(source, target, staged, in_sems, out_sems):
    pieces = in_sems.shape[0]
    rows = source.shape[0] // pieces
    places = [pl.ds(piece * rows, rows) for piece in range(pieces)]
    entering = [
        pltpu.make_async_copy(source.at[place, :], staged.at[place, :], in_sems.at[piece])
        for piece, place in enumerate(places)
    ]
    leaving = [
        pltpu.make_async_copy(staged.at[place, :], target.at[place, :], out_sems.at[piece])
        for piece, place in enumerate(places)
    ]
    for copy in entering:
        copy.start()
    for arrived, copy in zip(entering, leaving):
        arrived.wait()
        copy.start()
    for copy in leaving:
        copy.wait()


def per_device(query_states, key_states, value_states, doc_lengths, slopes):
    rows, all_columns = query_states.shape
    width = all_columns // slopes.shape[0]
    inner_count = lax.axis_size("inner")
    plane_groups = DOC_MAX // (rows * inner_count)
    slots = plane_groups * inner_count
    planes = lax.axis_size("outer") // plane_groups
    heads = slopes.shape[0] // slots
    blocks = DOC_MAX // BLOCK
    dtype = query_states.dtype
    gathered = pl.pallas_call(
        functools.partial(kernel, plane_groups, inner_count, planes, heads, width),
        out_shape=jax.ShapeDtypeStruct((rows, all_columns), dtype),
        in_specs=[pl.BlockSpec(memory_space=pltpu.HBM)] * 5,
        out_specs=pl.BlockSpec(memory_space=pltpu.HBM),
        scratch_shapes=[
            pltpu.SMEM(doc_lengths.shape, doc_lengths.dtype),
            pltpu.SMEM(slopes.shape, slopes.dtype),
            pltpu.VMEM((2 * DOC_MAX, heads * width), dtype),
            pltpu.VMEM((heads, DOC_MAX, width), dtype),
            pltpu.VMEM((heads, DOC_MAX, width), dtype),
            pltpu.VMEM((width, DOC_MAX), dtype),
            pltpu.VMEM((heads, DOC_MAX, width), dtype),
            pltpu.VMEM((heads, blocks, width, BLOCK), dtype),
            pltpu.VMEM((heads, blocks, width, BLOCK), dtype),
            pltpu.VMEM((heads, blocks, 1, BLOCK), jnp.float32),
            pltpu.VMEM((heads, blocks, 1, BLOCK), jnp.float32),
            pltpu.VMEM((width, DOC_MAX), jnp.float32),
            pltpu.VMEM((heads, 1, DOC_MAX), jnp.float32),
            pltpu.VMEM((heads, 1, DOC_MAX), jnp.float32),
            pltpu.VMEM((blocks * (blocks + 1) // 2 * BLOCK, BLOCK), dtype),
            pltpu.VMEM((blocks * (blocks + 1) // 2 * BLOCK, BLOCK), dtype),
            pltpu.VMEM((1, DOC_MAX), jnp.float32),
            pltpu.VMEM((1, 2 * DOC_MAX), jnp.float32),
            pltpu.VMEM((DOC_MAX, BLOCK), jnp.float32),
            pltpu.SemaphoreType.DMA((2,)),
            pltpu.SemaphoreType.DMA((3,)),
            pltpu.SemaphoreType.DMA((3, heads)),
            pltpu.SemaphoreType.DMA((3, heads, blocks)),
            pltpu.SemaphoreType.DMA((3, heads, blocks)),
            pltpu.SemaphoreType.DMA,
            pltpu.SemaphoreType.DMA,
        ],
        compiler_params=pltpu.CompilerParams(
            collective_id=0, has_side_effects=True, vmem_limit_bytes=64 * 1024 * 1024
        ),
        cost_estimate=pl.CostEstimate(
            flops=4 * heads * DOC_MAX * (DOC_MAX + BLOCK) * width,
            bytes_accessed=8 * rows * all_columns,
            transcendentals=heads * DOC_MAX * (DOC_MAX + BLOCK),
        ),
    )(doc_lengths, slopes, query_states, key_states, value_states)
    return pl.pallas_call(
        settle,
        out_shape=jax.ShapeDtypeStruct((rows, all_columns), dtype),
        in_specs=[pl.BlockSpec(memory_space=pl.ANY)],
        out_specs=pl.BlockSpec(memory_space=pl.ANY),
        scratch_shapes=[
            pltpu.VMEM((rows, all_columns), dtype),
            pltpu.SemaphoreType.DMA((8,)),
            pltpu.SemaphoreType.DMA((8,)),
        ],
        compiler_params=pltpu.CompilerParams(vmem_limit_bytes=64 * 1024 * 1024),
    )(gathered)


def solution(mesh):
    placed = P(("outer", "inner"), None)
    return jax.shard_map(
        per_device,
        mesh=mesh,
        in_specs=(placed, placed, placed, P(), P()),
        out_specs=placed,
        check_vma=False,
    )
```

```python
import functools
import math

import jax
import jax.numpy as jnp
from jax import lax
from jax.experimental import pallas as pl
from jax.experimental.pallas import tpu as pltpu
from jax.sharding import PartitionSpec as P

DOC_MAX = 1024
BLOCK = 256
NEG_FILL = -1e30
LOG2E = math.log2(math.e)
MESH = pl.DeviceIdType.MESH


def kernel(
    plane_groups, inner_count, planes, heads, width,
    doc_hbm, slope_hbm, q_ref, k_ref, v_ref, out_ref,
    doc_ref, slope_ref, q_buf, k_buf, v_buf, vt_buf, o_buf,
    far_out, far_in, lse_out, lse_in, near_sum, near_max, near_total, far_weights, near_weights, far_inverse, start_buf, pos_buf,
    small_sem, in_send, in_recv, z_send, z_recv, out_send, out_recv,
):
    rows = q_ref.shape[0]
    slots = plane_groups * inner_count
    outer = lax.axis_index("outer")
    inner = lax.axis_index("inner")
    plane = outer // plane_groups
    slot = (outer % plane_groups) * inner_count + inner
    has_prev = plane > 0
    has_next = plane < planes - 1
    prev_id = {"outer": outer - plane_groups, "inner": inner}
    next_id = {"outer": outer + plane_groups, "inner": inner}

    def device_of(peer):
        return {"outer": plane * plane_groups + peer // inner_count, "inner": peer % inner_count}

    peers = [(slot + step) % slots for step in range(1, slots)]

    def columns(owner, head):
        return pl.ds(pl.multiple_of((owner * heads + head) * width, width), width)

    own_rows = pl.ds(pl.multiple_of(slot * rows, rows), rows)

    small = [
        pltpu.make_async_copy(doc_hbm, doc_ref, small_sem.at[0]),
        pltpu.make_async_copy(slope_hbm, slope_ref, small_sem.at[1]),
    ]
    for copy in small:
        copy.start()

    barrier = pltpu.get_barrier_semaphore()
    for peer in peers:
        pl.semaphore_signal(barrier, inc=1, device_id=device_of(peer), device_id_type=MESH)

    @pl.when(has_prev)
    def _():
        pl.semaphore_signal(barrier, inc=1, device_id=prev_id, device_id_type=MESH)

    @pl.when(has_next)
    def _():
        pl.semaphore_signal(barrier, inc=1, device_id=next_id, device_id_type=MESH)

    pl.semaphore_wait(barrier, slots - 1 + has_prev.astype(jnp.int32) + has_next.astype(jnp.int32))

    def exchange(kind, source, target, head):
        for peer in peers:
            pltpu.make_async_remote_copy(
                src_ref=source.at[:, columns(peer, head)],
                dst_ref=target.at[head, own_rows, :],
                send_sem=in_send.at[kind],
                recv_sem=in_recv.at[kind, head],
                device_id=device_of(peer),
                device_id_type=MESH,
            ).start()
        pltpu.make_async_copy(
            source.at[:, columns(slot, head)], target.at[head, own_rows, :], in_recv.at[kind, head]
        ).start()

    for head in range(heads):
        exchange(0, q_ref, q_buf, head)
    for head in range(heads):
        exchange(1, k_ref, k_buf, head)
        exchange(2, v_ref, v_buf, head)

    for copy in small:
        copy.wait()

    position = plane * DOC_MAX + lax.broadcasted_iota(jnp.int32, (1, 2 * DOC_MAX), 1)

    def next_document(index, carry):
        end, start = carry
        end = end + doc_ref[index]
        return end, jnp.where(position >= end, end, start)

    start = lax.fori_loop(
        0, doc_ref.shape[0], next_document, (jnp.int32(0), jnp.zeros((1, 2 * DOC_MAX), jnp.int32))
    )[1]
    start_buf[...] = (start - plane * DOC_MAX).astype(jnp.float32)
    pos_buf[...] = lax.broadcasted_iota(jnp.int32, (DOC_MAX, BLOCK), 0).astype(jnp.float32)

    def whole(ref, sem):
        return pltpu.make_async_copy(ref, ref, sem)

    def z_copy(kind, head, index, source, target, device_id):
        return pltpu.make_async_remote_copy(
            src_ref=source,
            dst_ref=target,
            send_sem=z_send.at[kind, head, index],
            recv_sem=z_recv.at[kind, head, index],
            device_id=device_id,
            device_id_type=MESH,
        )

    scale = LOG2E / math.sqrt(width)
    blocks = DOC_MAX // BLOCK

    def score(head, query_first, key_first, key_count, slope, shift):
        keys = k_buf[head, pl.ds(key_first, key_count), :]
        query = q_buf[head, pl.ds(query_first, BLOCK), :]
        product = lax.dot_general(
            keys, query, (((1,), (1,)), ((), ())), preferred_element_type=jnp.float32
        )
        key_pos = pos_buf[pl.ds(key_first, key_count), :]
        allowed = key_pos >= start_buf[:, pl.ds(query_first, BLOCK)]
        return product * scale + (slope * key_pos + shift), allowed

    def weighted(key_first, key_count, weights):
        return jnp.dot(
            vt_buf[:, pl.ds(key_first, key_count)], weights, preferred_element_type=jnp.float32
        )

    def far_place(index):
        return pl.ds(index * DOC_MAX - index * (index - 1) // 2 * BLOCK, DOC_MAX - index * BLOCK)

    def near_place(index):
        return index * (index + 1) // 2 * BLOCK

    def far_weigh(head, slope):
        for index in range(blocks):
            first, count = index * BLOCK, DOC_MAX - index * BLOCK
            scores, allowed = score(head, DOC_MAX + first, first, count, slope, -DOC_MAX * slope)
            scores = jnp.where(allowed, scores, NEG_FILL)
            row_max = jnp.max(scores, axis=0, keepdims=True)
            weights = jnp.exp2(scores - row_max)
            row_total = jnp.sum(weights, axis=0, keepdims=True)
            far_weights[far_place(index), :] = weights.astype(far_weights.dtype)
            far_inverse[:, pl.ds(first, BLOCK)] = 1.0 / row_total
            lse_out[head, index] = row_max + jnp.log2(row_total)

    def far_send(head):
        for index in range(blocks):
            first, count = index * BLOCK, DOC_MAX - index * BLOCK
            part = weighted(first, count, far_weights[far_place(index), :])
            part = part * far_inverse[:, pl.ds(first, BLOCK)]
            far_out[head, index] = part.astype(far_out.dtype)
            z_copy(1, head, index, far_out.at[head, index], far_in.at[head, index], next_id).start()
            z_copy(2, head, index, lse_out.at[head, index], lse_in.at[head, index], next_id).start()

    def near_weigh(head, slope):
        for index in range(blocks):
            first, place = index * BLOCK, near_place(index)
            scores, allowed = score(head, first, first, BLOCK, slope, 0.0)
            causal = lax.broadcasted_iota(jnp.int32, (BLOCK, BLOCK), 0) <= (
                lax.broadcasted_iota(jnp.int32, (BLOCK, BLOCK), 1)
            )
            pieces = [(place + first, BLOCK, jnp.where(allowed & causal, scores, NEG_FILL))]
            if index:
                scores, allowed = score(head, first, 0, first, slope, 0.0)
                pieces.append((place, first, jnp.where(allowed, scores, NEG_FILL)))
            row_max = functools.reduce(
                jnp.maximum, [jnp.max(piece, axis=0, keepdims=True) for _, _, piece in pieces]
            )
            row_total = 0.0
            for piece_first, count, piece in pieces:
                weights = jnp.exp2(piece - row_max)
                row_total = row_total + jnp.sum(weights, axis=0, keepdims=True)
                near_weights[pl.ds(piece_first, count), :] = weights.astype(near_weights.dtype)
            near_max[head, :, pl.ds(first, BLOCK)] = row_max
            near_total[head, :, pl.ds(first, BLOCK)] = row_total

    def near_add():
        for index in range(blocks):
            count = (index + 1) * BLOCK
            weights = near_weights[pl.ds(near_place(index), count), :]
            near_sum[:, pl.ds(index * BLOCK, BLOCK)] = weighted(0, count, weights)

    def send_home(head, index):
        for part in range(BLOCK // rows):
            peer = index * (BLOCK // rows) + part
            done_rows = o_buf.at[head, pl.ds(peer * rows, rows), :]

            @pl.when(peer != slot)
            def _():
                pltpu.make_async_remote_copy(
                    src_ref=done_rows,
                    dst_ref=out_ref.at[:, columns(slot, head)],
                    send_sem=out_send,
                    recv_sem=out_recv,
                    device_id=device_of(peer),
                    device_id_type=MESH,
                ).start()

            @pl.when(peer == slot)
            def _():
                pltpu.make_async_copy(
                    done_rows, out_ref.at[:, columns(slot, head)], out_recv
                ).start()

    def finish_merged(head):
        for index in range(blocks):
            part = pl.ds(index * BLOCK, BLOCK)
            whole(far_in.at[head, index], z_recv.at[1, head, index]).wait()
            whole(lse_in.at[head, index], z_recv.at[2, head, index]).wait()
            far_lse = lse_in[head, index]
            top = jnp.maximum(near_max[head, :, part], far_lse)
            near_scale = jnp.exp2(near_max[head, :, part] - top)
            far_scale = jnp.exp2(far_lse - top)
            inverse = 1.0 / (near_total[head, :, part] * near_scale + far_scale)
            merged = near_sum[:, part] * (near_scale * inverse)
            merged = merged + far_in[head, index].astype(jnp.float32) * (far_scale * inverse)
            o_buf[head, part, :] = merged.T.astype(o_buf.dtype)
            send_home(head, index)

    def finish_alone(head):
        for index in range(blocks):
            part = pl.ds(index * BLOCK, BLOCK)
            alone = near_sum[:, part] / near_total[head, :, part]
            o_buf[head, part, :] = alone.T.astype(o_buf.dtype)
            send_home(head, index)

    def queries_back(head, unused):
        whole(q_buf.at[head, pl.ds(0, DOC_MAX), :], in_recv.at[0, head]).wait()

        @pl.when(has_prev)
        def _():
            z_copy(
                0, head, 0,
                q_buf.at[head, pl.ds(0, DOC_MAX), :],
                q_buf.at[head, pl.ds(DOC_MAX, DOC_MAX), :],
                prev_id,
            ).start()

        return unused

    lax.fori_loop(0, heads, queries_back, 0)

    def one_head(head, unused):
        slope = slope_ref[slot * heads + head] * LOG2E
        whole(k_buf.at[head], in_recv.at[1, head]).wait()

        @pl.when(has_next)
        def _():
            whole(q_buf.at[head, pl.ds(DOC_MAX, DOC_MAX), :], z_recv.at[0, head, 0]).wait()
            far_weigh(head, slope)

        near_weigh(head, slope)
        whole(v_buf.at[head], in_recv.at[2, head]).wait()
        vt_buf[...] = v_buf[head].T

        @pl.when(has_next)
        def _():
            far_send(head)

        @pl.when(has_prev & (head > 0))
        def _():
            finish_merged(head - 1)

        near_add()

        @pl.when(jnp.logical_not(has_prev))
        def _():
            finish_alone(head)

        return unused

    lax.fori_loop(0, heads, one_head, 0)

    @pl.when(has_prev)
    def _():
        finish_merged(heads - 1)

    sent = pl.ds(0, (slots - 1) * heads * width)
    for kind, source in enumerate((q_ref, k_ref, v_ref)):
        whole(source.at[:, sent], in_send.at[kind]).wait()
    whole(out_ref.at[:, sent], out_send).wait()
    for head in range(heads):

        @pl.when(has_prev)
        def _():
            whole(q_buf.at[head, pl.ds(0, DOC_MAX), :], z_send.at[0, head, 0]).wait()

        @pl.when(has_next)
        def _():
            for index in range(blocks):
                whole(far_out.at[head, index], z_send.at[1, head, index]).wait()
                whole(lse_out.at[head, index], z_send.at[2, head, index]).wait()

    whole(out_ref, out_recv).wait()


def settle(source, target, staged, in_sems, out_sems):
    pieces = in_sems.shape[0]
    rows = source.shape[0] // pieces
    places = [pl.ds(piece * rows, rows) for piece in range(pieces)]
    entering = [
        pltpu.make_async_copy(source.at[place, :], staged.at[place, :], in_sems.at[piece])
        for piece, place in enumerate(places)
    ]
    leaving = [
        pltpu.make_async_copy(staged.at[place, :], target.at[place, :], out_sems.at[piece])
        for piece, place in enumerate(places)
    ]
    for copy in entering:
        copy.start()
    for arrived, copy in zip(entering, leaving):
        arrived.wait()
        copy.start()
    for copy in leaving:
        copy.wait()


def per_device(query_states, key_states, value_states, doc_lengths, slopes):
    rows, all_columns = query_states.shape
    width = all_columns // slopes.shape[0]
    inner_count = lax.axis_size("inner")
    plane_groups = DOC_MAX // (rows * inner_count)
    slots = plane_groups * inner_count
    planes = lax.axis_size("outer") // plane_groups
    heads = slopes.shape[0] // slots
    blocks = DOC_MAX // BLOCK
    dtype = query_states.dtype
    gathered = pl.pallas_call(
        functools.partial(kernel, plane_groups, inner_count, planes, heads, width),
        out_shape=jax.ShapeDtypeStruct((rows, all_columns), dtype),
        in_specs=[pl.BlockSpec(memory_space=pltpu.HBM)] * 5,
        out_specs=pl.BlockSpec(memory_space=pltpu.HBM),
        scratch_shapes=[
            pltpu.SMEM(doc_lengths.shape, doc_lengths.dtype),
            pltpu.SMEM(slopes.shape, slopes.dtype),
            pltpu.VMEM((heads, 2 * DOC_MAX, width), dtype),
            pltpu.VMEM((heads, DOC_MAX, width), dtype),
            pltpu.VMEM((heads, DOC_MAX, width), dtype),
            pltpu.VMEM((width, DOC_MAX), dtype),
            pltpu.VMEM((heads, DOC_MAX, width), dtype),
            pltpu.VMEM((heads, blocks, width, BLOCK), dtype),
            pltpu.VMEM((heads, blocks, width, BLOCK), dtype),
            pltpu.VMEM((heads, blocks, 1, BLOCK), jnp.float32),
            pltpu.VMEM((heads, blocks, 1, BLOCK), jnp.float32),
            pltpu.VMEM((width, DOC_MAX), jnp.float32),
            pltpu.VMEM((heads, 1, DOC_MAX), jnp.float32),
            pltpu.VMEM((heads, 1, DOC_MAX), jnp.float32),
            pltpu.VMEM((blocks * (blocks + 1) // 2 * BLOCK, BLOCK), dtype),
            pltpu.VMEM((blocks * (blocks + 1) // 2 * BLOCK, BLOCK), dtype),
            pltpu.VMEM((1, DOC_MAX), jnp.float32),
            pltpu.VMEM((1, 2 * DOC_MAX), jnp.float32),
            pltpu.VMEM((DOC_MAX, BLOCK), jnp.float32),
            pltpu.SemaphoreType.DMA((2,)),
            pltpu.SemaphoreType.DMA((3,)),
            pltpu.SemaphoreType.DMA((3, heads)),
            pltpu.SemaphoreType.DMA((3, heads, blocks)),
            pltpu.SemaphoreType.DMA((3, heads, blocks)),
            pltpu.SemaphoreType.DMA,
            pltpu.SemaphoreType.DMA,
        ],
        compiler_params=pltpu.CompilerParams(
            collective_id=0, has_side_effects=True, vmem_limit_bytes=64 * 1024 * 1024
        ),
        cost_estimate=pl.CostEstimate(
            flops=4 * heads * DOC_MAX * (DOC_MAX + BLOCK) * width,
            bytes_accessed=8 * rows * all_columns,
            transcendentals=heads * DOC_MAX * (DOC_MAX + BLOCK),
        ),
    )(doc_lengths, slopes, query_states, key_states, value_states)
    return pl.pallas_call(
        settle,
        out_shape=jax.ShapeDtypeStruct((rows, all_columns), dtype),
        in_specs=[pl.BlockSpec(memory_space=pl.ANY)],
        out_specs=pl.BlockSpec(memory_space=pl.ANY),
        scratch_shapes=[
            pltpu.VMEM((rows, all_columns), dtype),
            pltpu.SemaphoreType.DMA((8,)),
            pltpu.SemaphoreType.DMA((8,)),
        ],
        compiler_params=pltpu.CompilerParams(vmem_limit_bytes=64 * 1024 * 1024),
    )(gathered)


def solution(mesh):
    placed = P(("outer", "inner"), None)
    return jax.shard_map(
        per_device,
        mesh=mesh,
        in_specs=(placed, placed, placed, P(), P()),
        out_specs=placed,
        check_vma=False,
    )
```

```python
import functools
import math

import jax
import jax.numpy as jnp
from jax import lax
from jax.experimental import pallas as pl
from jax.experimental.pallas import tpu as pltpu
from jax.sharding import PartitionSpec as P

DOC_MAX = 1024
BLOCK = 256
NEG_FILL = -1e30
LOG2E = math.log2(math.e)
MESH = pl.DeviceIdType.MESH


def kernel(
    plane_groups, inner_count, planes, heads, width,
    doc_hbm, slope_hbm, q_ref, k_ref, v_ref, out_ref,
    doc_ref, slope_ref, q_buf, k_buf, v_buf, vt_buf, o_buf,
    far_out, far_in, lse_out, lse_in, near_sum, near_max, near_total, far_weights, near_weights, far_inverse, start_buf, pos_buf,
    small_sem, in_send, in_recv, z_send, z_recv, out_send, out_recv,
):
    rows = q_ref.shape[0]
    slots = plane_groups * inner_count
    outer = lax.axis_index("outer")
    inner = lax.axis_index("inner")
    plane = outer // plane_groups
    slot = (outer % plane_groups) * inner_count + inner
    has_prev = plane > 0
    has_next = plane < planes - 1
    prev_id = {"outer": outer - plane_groups, "inner": inner}
    next_id = {"outer": outer + plane_groups, "inner": inner}

    def device_of(peer):
        return {"outer": plane * plane_groups + peer // inner_count, "inner": peer % inner_count}

    peers = [(slot + step) % slots for step in range(1, slots)]

    def columns(owner, head):
        return pl.ds(pl.multiple_of((owner * heads + head) * width, width), width)

    own_rows = pl.ds(pl.multiple_of(slot * rows, rows), rows)

    small = [
        pltpu.make_async_copy(doc_hbm, doc_ref, small_sem.at[0]),
        pltpu.make_async_copy(slope_hbm, slope_ref, small_sem.at[1]),
    ]
    for copy in small:
        copy.start()

    barrier = pltpu.get_barrier_semaphore()
    for peer in peers:
        pl.semaphore_signal(barrier, inc=1, device_id=device_of(peer), device_id_type=MESH)

    @pl.when(has_prev)
    def _():
        pl.semaphore_signal(barrier, inc=1, device_id=prev_id, device_id_type=MESH)

    @pl.when(has_next)
    def _():
        pl.semaphore_signal(barrier, inc=1, device_id=next_id, device_id_type=MESH)

    pl.semaphore_wait(barrier, slots - 1 + has_prev.astype(jnp.int32) + has_next.astype(jnp.int32))

    def exchange(kind, source, target, head):
        for peer in peers:
            pltpu.make_async_remote_copy(
                src_ref=source.at[:, columns(peer, head)],
                dst_ref=target.at[head, own_rows, :],
                send_sem=in_send.at[kind],
                recv_sem=in_recv.at[kind, head],
                device_id=device_of(peer),
                device_id_type=MESH,
            ).start()
        pltpu.make_async_copy(
            source.at[:, columns(slot, head)], target.at[head, own_rows, :], in_recv.at[kind, head]
        ).start()

    ahead = min(2, heads)
    for head in range(ahead):
        exchange(0, q_ref, q_buf, head)
    for head in range(heads):
        if head + ahead < heads:
            exchange(0, q_ref, q_buf, head + ahead)
        exchange(1, k_ref, k_buf, head)
        exchange(2, v_ref, v_buf, head)

    for copy in small:
        copy.wait()

    position = plane * DOC_MAX + lax.broadcasted_iota(jnp.int32, (1, 2 * DOC_MAX), 1)

    def next_document(index, carry):
        end, start = carry
        end = end + doc_ref[index]
        return end, jnp.where(position >= end, end, start)

    start = lax.fori_loop(
        0, doc_ref.shape[0], next_document, (jnp.int32(0), jnp.zeros((1, 2 * DOC_MAX), jnp.int32))
    )[1]
    start_buf[...] = (start - plane * DOC_MAX).astype(jnp.float32)
    pos_buf[...] = lax.broadcasted_iota(jnp.int32, (DOC_MAX, BLOCK), 0).astype(jnp.float32)

    def whole(ref, sem):
        return pltpu.make_async_copy(ref, ref, sem)

    def z_copy(kind, head, index, source, target, device_id):
        return pltpu.make_async_remote_copy(
            src_ref=source,
            dst_ref=target,
            send_sem=z_send.at[kind, head, index],
            recv_sem=z_recv.at[kind, head, index],
            device_id=device_id,
            device_id_type=MESH,
        )

    scale = LOG2E / math.sqrt(width)
    blocks = DOC_MAX // BLOCK

    def score(head, query_first, key_first, key_count, slope, shift):
        keys = k_buf[head, pl.ds(key_first, key_count), :]
        query = q_buf[head, pl.ds(query_first, BLOCK), :]
        product = lax.dot_general(
            keys, query, (((1,), (1,)), ((), ())), preferred_element_type=jnp.float32
        )
        key_pos = pos_buf[pl.ds(key_first, key_count), :]
        allowed = key_pos >= start_buf[:, pl.ds(query_first, BLOCK)]
        return product * scale + (slope * key_pos + shift), allowed

    def weighted(key_first, key_count, weights):
        return jnp.dot(
            vt_buf[:, pl.ds(key_first, key_count)], weights, preferred_element_type=jnp.float32
        )

    def far_place(index):
        return pl.ds(index * DOC_MAX - index * (index - 1) // 2 * BLOCK, DOC_MAX - index * BLOCK)

    def near_place(index):
        return index * (index + 1) // 2 * BLOCK

    def far_weigh(head, slope):
        for index in range(blocks):
            first, count = index * BLOCK, DOC_MAX - index * BLOCK
            scores, allowed = score(head, DOC_MAX + first, first, count, slope, -DOC_MAX * slope)
            scores = jnp.where(allowed, scores, NEG_FILL)
            row_max = jnp.max(scores, axis=0, keepdims=True)
            weights = jnp.exp2(scores - row_max)
            row_total = jnp.sum(weights, axis=0, keepdims=True)
            far_weights[far_place(index), :] = weights.astype(far_weights.dtype)
            far_inverse[:, pl.ds(first, BLOCK)] = 1.0 / row_total
            lse_out[head, index] = row_max + jnp.log2(row_total)

    def far_send(head):
        for index in range(blocks):
            first, count = index * BLOCK, DOC_MAX - index * BLOCK
            part = weighted(first, count, far_weights[far_place(index), :])
            part = part * far_inverse[:, pl.ds(first, BLOCK)]
            far_out[head, index] = part.astype(far_out.dtype)
            z_copy(1, head, index, far_out.at[head, index], far_in.at[head, index], next_id).start()
            z_copy(2, head, index, lse_out.at[head, index], lse_in.at[head, index], next_id).start()

    def near_weigh(head, slope):
        for index in range(blocks):
            first, place = index * BLOCK, near_place(index)
            scores, allowed = score(head, first, first, BLOCK, slope, 0.0)
            causal = lax.broadcasted_iota(jnp.int32, (BLOCK, BLOCK), 0) <= (
                lax.broadcasted_iota(jnp.int32, (BLOCK, BLOCK), 1)
            )
            pieces = [(place + first, BLOCK, jnp.where(allowed & causal, scores, NEG_FILL))]
            if index:
                scores, allowed = score(head, first, 0, first, slope, 0.0)
                pieces.append((place, first, jnp.where(allowed, scores, NEG_FILL)))
            row_max = functools.reduce(
                jnp.maximum, [jnp.max(piece, axis=0, keepdims=True) for _, _, piece in pieces]
            )
            row_total = 0.0
            for piece_first, count, piece in pieces:
                weights = jnp.exp2(piece - row_max)
                row_total = row_total + jnp.sum(weights, axis=0, keepdims=True)
                near_weights[pl.ds(piece_first, count), :] = weights.astype(near_weights.dtype)
            near_max[head, :, pl.ds(first, BLOCK)] = row_max
            near_total[head, :, pl.ds(first, BLOCK)] = row_total

    def near_add():
        for index in range(blocks):
            count = (index + 1) * BLOCK
            weights = near_weights[pl.ds(near_place(index), count), :]
            near_sum[:, pl.ds(index * BLOCK, BLOCK)] = weighted(0, count, weights)

    def send_home(head, index):
        for part in range(BLOCK // rows):
            peer = index * (BLOCK // rows) + part
            done_rows = o_buf.at[head, pl.ds(peer * rows, rows), :]

            @pl.when(peer != slot)
            def _():
                pltpu.make_async_remote_copy(
                    src_ref=done_rows,
                    dst_ref=out_ref.at[:, columns(slot, head)],
                    send_sem=out_send,
                    recv_sem=out_recv,
                    device_id=device_of(peer),
                    device_id_type=MESH,
                ).start()

            @pl.when(peer == slot)
            def _():
                pltpu.make_async_copy(
                    done_rows, out_ref.at[:, columns(slot, head)], out_recv
                ).start()

    def finish_merged(head):
        for index in range(blocks):
            part = pl.ds(index * BLOCK, BLOCK)
            whole(far_in.at[head, index], z_recv.at[1, head, index]).wait()
            whole(lse_in.at[head, index], z_recv.at[2, head, index]).wait()
            far_lse = lse_in[head, index]
            top = jnp.maximum(near_max[head, :, part], far_lse)
            near_scale = jnp.exp2(near_max[head, :, part] - top)
            far_scale = jnp.exp2(far_lse - top)
            inverse = 1.0 / (near_total[head, :, part] * near_scale + far_scale)
            merged = near_sum[:, part] * (near_scale * inverse)
            merged = merged + far_in[head, index].astype(jnp.float32) * (far_scale * inverse)
            o_buf[head, part, :] = merged.T.astype(o_buf.dtype)
            send_home(head, index)

    def finish_alone(head):
        for index in range(blocks):
            part = pl.ds(index * BLOCK, BLOCK)
            alone = near_sum[:, part] / near_total[head, :, part]
            o_buf[head, part, :] = alone.T.astype(o_buf.dtype)
            send_home(head, index)

    def queries_back(head, unused):
        whole(q_buf.at[head, pl.ds(0, DOC_MAX), :], in_recv.at[0, head]).wait()

        @pl.when(has_prev)
        def _():
            z_copy(
                0, head, 0,
                q_buf.at[head, pl.ds(0, DOC_MAX), :],
                q_buf.at[head, pl.ds(DOC_MAX, DOC_MAX), :],
                prev_id,
            ).start()

        return unused

    lax.fori_loop(0, ahead, queries_back, 0)

    def one_head(head, unused):
        slope = slope_ref[slot * heads + head] * LOG2E
        @pl.when(head + ahead < heads)
        def _():
            queries_back(head + ahead, 0)

        whole(k_buf.at[head], in_recv.at[1, head]).wait()

        @pl.when(has_next)
        def _():
            whole(q_buf.at[head, pl.ds(DOC_MAX, DOC_MAX), :], z_recv.at[0, head, 0]).wait()
            far_weigh(head, slope)

        near_weigh(head, slope)
        whole(v_buf.at[head], in_recv.at[2, head]).wait()
        vt_buf[...] = v_buf[head].T

        @pl.when(has_next)
        def _():
            far_send(head)

        @pl.when(has_prev & (head > 0))
        def _():
            finish_merged(head - 1)

        near_add()

        @pl.when(jnp.logical_not(has_prev))
        def _():
            finish_alone(head)

        return unused

    lax.fori_loop(0, heads, one_head, 0)

    @pl.when(has_prev)
    def _():
        finish_merged(heads - 1)

    sent = pl.ds(0, (slots - 1) * heads * width)
    for kind, source in enumerate((q_ref, k_ref, v_ref)):
        whole(source.at[:, sent], in_send.at[kind]).wait()
    whole(out_ref.at[:, sent], out_send).wait()
    for head in range(heads):

        @pl.when(has_prev)
        def _():
            whole(q_buf.at[head, pl.ds(0, DOC_MAX), :], z_send.at[0, head, 0]).wait()

        @pl.when(has_next)
        def _():
            for index in range(blocks):
                whole(far_out.at[head, index], z_send.at[1, head, index]).wait()
                whole(lse_out.at[head, index], z_send.at[2, head, index]).wait()

    whole(out_ref, out_recv).wait()


def settle(source, target, staged, in_sems, out_sems):
    pieces = in_sems.shape[0]
    rows = source.shape[0] // pieces
    places = [pl.ds(piece * rows, rows) for piece in range(pieces)]
    entering = [
        pltpu.make_async_copy(source.at[place, :], staged.at[place, :], in_sems.at[piece])
        for piece, place in enumerate(places)
    ]
    leaving = [
        pltpu.make_async_copy(staged.at[place, :], target.at[place, :], out_sems.at[piece])
        for piece, place in enumerate(places)
    ]
    for copy in entering:
        copy.start()
    for arrived, copy in zip(entering, leaving):
        arrived.wait()
        copy.start()
    for copy in leaving:
        copy.wait()


def per_device(query_states, key_states, value_states, doc_lengths, slopes):
    rows, all_columns = query_states.shape
    width = all_columns // slopes.shape[0]
    inner_count = lax.axis_size("inner")
    plane_groups = DOC_MAX // (rows * inner_count)
    slots = plane_groups * inner_count
    planes = lax.axis_size("outer") // plane_groups
    heads = slopes.shape[0] // slots
    blocks = DOC_MAX // BLOCK
    dtype = query_states.dtype
    gathered = pl.pallas_call(
        functools.partial(kernel, plane_groups, inner_count, planes, heads, width),
        out_shape=jax.ShapeDtypeStruct((rows, all_columns), dtype),
        in_specs=[pl.BlockSpec(memory_space=pltpu.HBM)] * 5,
        out_specs=pl.BlockSpec(memory_space=pltpu.HBM),
        scratch_shapes=[
            pltpu.SMEM(doc_lengths.shape, doc_lengths.dtype),
            pltpu.SMEM(slopes.shape, slopes.dtype),
            pltpu.VMEM((heads, 2 * DOC_MAX, width), dtype),
            pltpu.VMEM((heads, DOC_MAX, width), dtype),
            pltpu.VMEM((heads, DOC_MAX, width), dtype),
            pltpu.VMEM((width, DOC_MAX), dtype),
            pltpu.VMEM((heads, DOC_MAX, width), dtype),
            pltpu.VMEM((heads, blocks, width, BLOCK), dtype),
            pltpu.VMEM((heads, blocks, width, BLOCK), dtype),
            pltpu.VMEM((heads, blocks, 1, BLOCK), jnp.float32),
            pltpu.VMEM((heads, blocks, 1, BLOCK), jnp.float32),
            pltpu.VMEM((width, DOC_MAX), jnp.float32),
            pltpu.VMEM((heads, 1, DOC_MAX), jnp.float32),
            pltpu.VMEM((heads, 1, DOC_MAX), jnp.float32),
            pltpu.VMEM((blocks * (blocks + 1) // 2 * BLOCK, BLOCK), dtype),
            pltpu.VMEM((blocks * (blocks + 1) // 2 * BLOCK, BLOCK), dtype),
            pltpu.VMEM((1, DOC_MAX), jnp.float32),
            pltpu.VMEM((1, 2 * DOC_MAX), jnp.float32),
            pltpu.VMEM((DOC_MAX, BLOCK), jnp.float32),
            pltpu.SemaphoreType.DMA((2,)),
            pltpu.SemaphoreType.DMA((3,)),
            pltpu.SemaphoreType.DMA((3, heads)),
            pltpu.SemaphoreType.DMA((3, heads, blocks)),
            pltpu.SemaphoreType.DMA((3, heads, blocks)),
            pltpu.SemaphoreType.DMA,
            pltpu.SemaphoreType.DMA,
        ],
        compiler_params=pltpu.CompilerParams(
            collective_id=0, has_side_effects=True, vmem_limit_bytes=64 * 1024 * 1024
        ),
        cost_estimate=pl.CostEstimate(
            flops=4 * heads * DOC_MAX * (DOC_MAX + BLOCK) * width,
            bytes_accessed=8 * rows * all_columns,
            transcendentals=heads * DOC_MAX * (DOC_MAX + BLOCK),
        ),
    )(doc_lengths, slopes, query_states, key_states, value_states)
    return pl.pallas_call(
        settle,
        out_shape=jax.ShapeDtypeStruct((rows, all_columns), dtype),
        in_specs=[pl.BlockSpec(memory_space=pl.ANY)],
        out_specs=pl.BlockSpec(memory_space=pl.ANY),
        scratch_shapes=[
            pltpu.VMEM((rows, all_columns), dtype),
            pltpu.SemaphoreType.DMA((8,)),
            pltpu.SemaphoreType.DMA((8,)),
        ],
        compiler_params=pltpu.CompilerParams(vmem_limit_bytes=64 * 1024 * 1024),
    )(gathered)


def solution(mesh):
    placed = P(("outer", "inner"), None)
    return jax.shard_map(
        per_device,
        mesh=mesh,
        in_specs=(placed, placed, placed, P(), P()),
        out_specs=placed,
        check_vma=False,
    )
```
